32 devices in a mesh: wide: 8 (over z, y), lev: 4 (over x, core).
Axes of the slice: x: 2, y: 2, z: 4, core: 2. Of those that a mesh axis runs over, the one named last changes fastest.
Arguments:
- nonlinear: bfloat16 [3, 2, 256, 8, 4096], P(None, None, 'lev', None, 'wide'), may hold values from -20 to 20
Outputs:
- pressure: float32 [2, 256, 8, 1536], P(None, 'lev', 'wide')
The draws below stay inside these ranges and needn't reach their ends.
All inputs are finite; a program needn't handle non-finite values.
Results may differ from the reference program's by a relative error of at most 0.0034.
Values may be sent and summed in bfloat16 or wider, within the bound.
A program may use at most 64 MiB of HBM per device.

```python
import math
import jax
import jax.numpy as jnp
from jax import lax

NXG = 4096
KXM = 1536
NKY = 8
NZ = 256


def draw_nonlinear(key, part):
    keys = jax.random.split(key, 6)
    full_shape = (3, 2, NZ, NKY, NXG)
    white = jax.random.truncated_normal(keys[0], -4.0, 4.0, full_shape, jnp.float32)
    line = jax.random.truncated_normal(keys[1], -4.0, 4.0, (2, NKY, NXG), jnp.float32)
    level_gain = jax.random.uniform(keys[2], (2, 1, NKY, 1), jnp.float32, 2.0, 4.0)
    alternate_gain = jax.random.uniform(keys[3], (2, 1, NKY, 1), jnp.float32, -1.0, 1.0)
    phase = jax.random.uniform(keys[4], (2, 1, NKY, 1), jnp.float32, -math.pi, math.pi)
    cycles = jax.random.randint(keys[5], (2, 1, NKY, 1), 0, 3).astype(jnp.float32)
    level_index = jnp.arange(NZ, dtype=jnp.int32)
    levels = level_index.astype(jnp.float32)[None, :, None, None]
    signs = (1 - 2 * jnp.mod(level_index, 2)).astype(jnp.float32)[None, :, None, None]
    profile = level_gain * (1.0 + 0.5 * jnp.cos(2.0 * math.pi * cycles * levels / NZ + phase)) + alternate_gain * signs
    slope = line - jnp.roll(line, 1, axis=2)
    structured = profile * slope[:, None]
    first_field = white[0] + structured
    whole = jnp.concatenate([first_field[None], white[1:]], axis=0)
    return jnp.clip(whole, -20.0, 20.0).astype(jnp.bfloat16)


def setup_inputs(seed: int = 0) -> dict:
    key_list = jax.random.split(jax.random.key(seed), 2)
    return {
        "nonlinear": draw_nonlinear(jax.random.fold_in(key_list[1], 71), 0),
    }


def make_tables():
    places = jnp.arange(NXG, dtype=jnp.int32)
    waves = jnp.arange(KXM, dtype=jnp.int32) - KXM // 2
    phases = jnp.mod(places[:, None] * waves[None, :], NXG).astype(jnp.int32)
    angles = phases.astype(jnp.float32) * (2.0 * math.pi / NXG)
    return (jnp.cos(angles).astype(jnp.bfloat16), jnp.sin(angles).astype(jnp.bfloat16))

def wave_scales(first_row, row_count):
    spacing = 2.0 * math.pi / NXG
    ky_scaled = (first_row + jnp.arange(row_count, dtype=jnp.int32)).astype(jnp.float32) * spacing
    kx_scaled = (jnp.arange(KXM, dtype=jnp.int32) - KXM // 2).astype(jnp.float32) * spacing
    return (ky_scaled[:, None], kx_scaled[None, :])

def vertical_mix(y_term, z_padded, ky_scaled):
    upper = z_padded[:, 2:].astype(jnp.float32)
    lower = z_padded[:, :-2].astype(jnp.float32)
    half_diff = (upper - lower) * 0.5
    y_wide = y_term.astype(jnp.float32)
    real_part = half_diff[0] - ky_scaled * y_wide[1]
    imag_part = half_diff[1] + ky_scaled * y_wide[0]
    return jnp.stack([real_part, imag_part]).astype(jnp.bfloat16)

def spectral_source(x_term, g_term, cosine, sine, kx_scaled):
    stacked = jnp.concatenate([x_term, g_term], axis=0)
    lead_shape = stacked.shape[:3]
    flat_rows = stacked.reshape(-1, stacked.shape[3])
    with_cos = jnp.dot(flat_rows, cosine, preferred_element_type=jnp.float32).reshape(lead_shape + (cosine.shape[1],))
    with_sin = jnp.dot(flat_rows, sine, preferred_element_type=jnp.float32).reshape(lead_shape + (sine.shape[1],))
    norm_scale = 1.0 / math.sqrt(cosine.shape[0])
    fx_real = (with_cos[0] + with_sin[1]) * norm_scale
    fx_imag = (with_cos[1] - with_sin[0]) * norm_scale
    fg_real = (with_cos[2] + with_sin[3]) * norm_scale
    fg_imag = (with_cos[3] - with_sin[2]) * norm_scale
    return jnp.stack([kx_scaled * fx_imag - fg_real, -kx_scaled * fx_real - fg_imag])

def tridiag_sweep(diagonal, source):

    def forward_step(previous, row_data):
        shift_coef, prior_value = previous
        inverse = 1.0 / (diagonal + shift_coef)
        reduced_value = (row_data + prior_value) * inverse
        return ((-inverse, reduced_value), (inverse, reduced_value))
    initial = (jnp.zeros_like(diagonal), jnp.zeros_like(source[0]))
    _, (inverses, reduced) = lax.scan(forward_step, initial, source)

    def backward_step(following, row_pair):
        inverse, reduced_value = row_pair
        result = reduced_value + inverse * following
        return (result, result)
    _, solved = lax.scan(backward_step, jnp.zeros_like(source[0]), (inverses, reduced), reverse=True)
    return solved

def reference(nonlinear):
    cosine, sine = make_tables()
    ky_scaled, kx_scaled = wave_scales(0, NKY)
    field_x = nonlinear[0]
    field_y = nonlinear[1]
    padded = jnp.pad(nonlinear[2], ((0, 0), (1, 1), (0, 0), (0, 0)))

    def level_source(level):
        x_level = lax.dynamic_slice_in_dim(field_x, level, 1, 1)
        y_level = lax.dynamic_slice_in_dim(field_y, level, 1, 1)
        z_level = lax.dynamic_slice_in_dim(padded, level, 3, 1)
        combined = vertical_mix(y_level, z_level, ky_scaled)
        return spectral_source(x_level, combined, cosine, sine, kx_scaled)[:, 0]
    source = lax.map(level_source, jnp.arange(NZ, dtype=jnp.int32))
    diagonal = 2.0 + (ky_scaled * ky_scaled + kx_scaled * kx_scaled)
    solved = tridiag_sweep(diagonal, source)
    return jnp.moveaxis(solved, 0, 1)
```

```python
import functools
import math

import jax
import jax.numpy as jnp
import ml_dtypes
import numpy as np
from jax import lax
from jax.experimental import pallas as pl
from jax.experimental.pallas import tpu as pltpu
from jax.sharding import PartitionSpec as P

NXG = 4096
KXM = 1536
MESH = pl.DeviceIdType.MESH
SEC = 512
TILE = 256
SECTIONS = KXM // SEC
PER = SEC // 128
DEEP = 2 * PER


def make_tables():
    places = np.arange(NXG, dtype=np.int32)
    waves = np.arange(KXM, dtype=np.int32) - KXM // 2
    phases = np.mod(places[:, None] * waves[None, :], NXG)
    turn = np.arange(NXG, dtype=np.float32) * np.float32(2.0 * math.pi / NXG)
    cosine = np.cos(turn).astype(ml_dtypes.bfloat16)[phases]
    sine = np.sin(turn).astype(ml_dtypes.bfloat16)[phases]
    return np.concatenate([cosine, sine], axis=1)


def level_rows(i, count=1):
    return pl.ds(pl.multiple_of(i * DEEP, DEEP), count * DEEP)


def kernel(
    wide, lev, rows_ky, levels,
    x_ref, tab_ref, out_ref,
    tab, send, recv, halo_lo, halo_hi, zpad, part, flow_out, flow_in, coef, from_lo,
    ends, last_val, first_val,
    tab_sem, halo_send, halo_recv, send_sem, recv_sem, flow_send, flow_recv, end_send, end_recv,
):
    f32, bf16 = jnp.float32, jnp.bfloat16
    chunk = x_ref.shape[3]
    line_rows = levels * rows_ky
    half = 2 * levels
    group_levels = max(16, 256 // rows_ky)
    group_rows = group_levels * rows_ky
    groups = levels // group_levels
    halo_rows = halo_lo.shape[1]
    spacing = 2.0 * math.pi / NXG
    me = lax.axis_index("wide")
    block = lax.axis_index("lev")
    chain = wide // 2
    q, h = me // 2, me % 2
    pair = me + 1 - 2 * h

    tab_parts = tab_sem.shape[1]
    tab_rows = chunk // tab_parts

    def tab_copy(side, i):
        owner = me if side == 0 else pair
        at = pl.multiple_of(owner * chunk + i * tab_rows, tab_rows)
        return pltpu.make_async_copy(
            tab_ref.at[pl.ds(at, tab_rows)],
            tab.at[pl.ds(side * chunk + i * tab_rows, tab_rows)],
            tab_sem.at[side, i],
        )

    barrier = pltpu.get_barrier_semaphore()
    pl.semaphore_signal(barrier, inc=1, device_id={"wide": pair}, device_id_type=MESH)

    @pl.when(q > 0)
    def _():
        pl.semaphore_signal(barrier, inc=1, device_id={"wide": me - 2}, device_id_type=MESH)

    @pl.when(q < chain - 1)
    def _():
        pl.semaphore_signal(barrier, inc=1, device_id={"wide": me + 2}, device_id_type=MESH)

    for step in range(1, lev):
        pl.semaphore_signal(
            barrier, inc=1, device_id={"lev": (block + step) % lev}, device_id_type=MESH
        )
    for side in range(2):
        for i in range(tab_parts):
            tab_copy(side, i).start()

    out_row = lax.broadcasted_iota(jnp.int32, (group_rows, group_rows), 0)
    in_row = lax.broadcasted_iota(jnp.int32, (group_rows, group_rows), 1)
    wanted = (out_row % group_levels) * rows_ky + out_row // group_levels
    shuffle = jnp.where(in_row == wanted, 1.0, 0.0).astype(bf16)

    def place(values, first):
        moved = jnp.dot(shuffle, values, preferred_element_type=f32).astype(bf16)
        for ky in range(rows_ky):
            send[ky, first:first + group_levels, :] = moved[
                ky * group_levels:(ky + 1) * group_levels
            ]

    upper_far = 1 - (2 * q) // chain
    far = upper_far * (chain - 1 - q) + (1 - upper_far) * q
    near_count = chain - 1 - far
    alone = far - near_count

    def unit(s):
        late = (s - alone + chain) // chain
        t = late * (s - alone)
        distance = (1 - late) * (far - s) + late * (near_count - t // 2)
        up = (1 - late) * upper_far + late * ((1 - upper_far) * (1 - t % 2) + upper_far * (t % 2))
        way = 2 * up - 1
        return q + way * distance, way

    def line_copy(d, which):
        rows = pl.ds(which * half, half)
        return pltpu.make_async_remote_copy(
            src_ref=send.at[2 * d + 1 - h, rows],
            dst_ref=recv.at[d, rows],
            send_sem=send_sem.at[which, d],
            recv_sem=recv_sem.at[which, d],
            device_id={"wide": pair},
            device_id_type=MESH,
        )

    for c in range(2):
        for g in range(groups):
            place(
                x_ref[0, c, g * group_rows:(g + 1) * group_rows, :],
                c * levels + g * group_levels,
            )
    has_prev = (q + chain - 1) // chain
    has_next = (2 * chain - 2 - q) // chain
    pl.semaphore_wait(barrier, lev + has_prev + has_next)

    to_prev = pltpu.make_async_remote_copy(
        src_ref=x_ref.at[2, :, 0:halo_rows],
        dst_ref=halo_hi,
        send_sem=halo_send.at[0],
        recv_sem=halo_recv.at[0],
        device_id={"lev": (block + lev - 1) % lev},
        device_id_type=MESH,
    )
    to_next = pltpu.make_async_remote_copy(
        src_ref=x_ref.at[2, :, line_rows - halo_rows:line_rows],
        dst_ref=halo_lo,
        send_sem=halo_send.at[1],
        recv_sem=halo_recv.at[1],
        device_id={"lev": (block + 1) % lev},
        device_id_type=MESH,
    )
    to_prev.start()
    to_next.start()
    first_unit, _ = unit(0)
    line_copy(first_unit, 0).start()

    for c in range(2):
        zpad[c, rows_ky:rows_ky + line_rows, :] = x_ref[2, c].astype(f32)
    to_prev.wait_recv()
    to_next.wait_recv()
    for c in range(2):
        low = halo_lo[c].astype(f32)[halo_rows - rows_ky:]
        high = halo_hi[c].astype(f32)[:rows_ky]
        zpad[c, 0:rows_ky, :] = jnp.where(block > 0, low, 0.0)
        zpad[c, rows_ky + line_rows:, :] = jnp.where(block < lev - 1, high, 0.0)
    ky_row = lax.broadcasted_iota(jnp.int32, (group_rows, chunk), 0) % rows_ky
    ky_scaled = ky_row.astype(f32) * spacing
    for c in range(2):
        for g in range(groups):
            at = g * group_rows
            upper = zpad[c, at + 2 * rows_ky:at + 2 * rows_ky + group_rows, :]
            lower = zpad[c, at:at + group_rows, :]
            turned = ky_scaled * x_ref[1, 1 - c, at:at + group_rows, :].astype(f32)
            slope = (upper - lower) * 0.5
            mixed = slope - turned if c == 0 else slope + turned
            place(mixed.astype(bf16), half + c * levels + g * group_levels)
    line_copy(first_unit, 1).start()

    def send_lines(s, carry):
        d, _ = unit(s)
        line_copy(d, 0).start()
        line_copy(d, 1).start()
        return carry

    lax.fori_loop(1, chain, send_lines, 0)

    def clear(slot):
        for k in range(SECTIONS):
            flow_in[slot, k] = jnp.zeros(flow_in.shape[2:], bf16)

    @pl.when(q == 0)
    def _():
        @pl.loop(0, chain)
        def _(slot):
            clear(slot)

    @pl.when(q == chain - 1)
    def _():
        @pl.loop(0, chain - 1)
        def _(slot):
            clear(slot)

        clear(chain)

    part_row = lax.broadcasted_iota(jnp.int32, (DEEP, 128), 0)
    lane = lax.broadcasted_iota(jnp.int32, (DEEP, 128), 1)

    def diagonal(ky, k):
        column = k * SEC + (part_row % PER) * 128 + lane
        kx = (column - KXM // 2).astype(f32) * spacing
        kyd = ky.astype(f32) * spacing
        return 2.0 + (kyd * kyd + kx * kx)

    own_diagonal = [diagonal(me, k) for k in range(SECTIONS)]

    def coef_step(i, carry):
        after = []
        for k in range(SECTIONS):
            shift, gain = carry[2 * k], carry[2 * k + 1]
            inverse = 1.0 / (own_diagonal[k] - shift)
            gain = gain * inverse
            coef[k, level_rows(i), :] = inverse
            from_lo[k, level_rows(i), :] = gain
            after += [inverse, gain]
        return tuple(after)

    zeros = jnp.zeros((DEEP, 128), f32)
    ones = jnp.ones((DEEP, 128), f32)
    lax.fori_loop(0, levels, coef_step, (zeros, ones) * SECTIONS)

    def unit_step(j, carry):
        i = levels - 1 - j
        after = []
        for k in range(SECTIONS):
            low = from_lo[k, level_rows(i), :] + coef[k, level_rows(i), :] * carry[k]
            from_lo[k, level_rows(i), :] = low
            after.append(low)
        return tuple(after)

    lax.fori_loop(0, levels, unit_step, (zeros,) * SECTIONS)

    for side in range(2):
        for i in range(tab_parts):
            tab_copy(side, i).wait()

    norm_scale = 1.0 / math.sqrt(NXG)

    def transform(d, k):
        lines = jnp.concatenate([send[2 * d + h], recv[d]], axis=1)
        for t in range(SEC // TILE):
            first = k * SEC + t * TILE
            with_cos = jnp.dot(lines, tab[:, first:first + TILE], preferred_element_type=f32)
            with_sin = jnp.dot(
                lines, tab[:, KXM + first:KXM + first + TILE], preferred_element_type=f32
            )
            kx = (
                lax.broadcasted_iota(jnp.int32, (1, TILE), 1) + first - KXM // 2
            ).astype(f32) * spacing
            n = levels
            fx_real = (with_cos[0:n] + with_sin[n:2 * n]) * norm_scale
            fx_imag = (with_cos[n:2 * n] - with_sin[0:n]) * norm_scale
            fg_real = (with_cos[2 * n:3 * n] + with_sin[3 * n:4 * n]) * norm_scale
            fg_imag = (with_cos[3 * n:4 * n] - with_sin[2 * n:3 * n]) * norm_scale
            source_real = kx * fx_imag - fg_real
            source_imag = -kx * fx_real - fg_imag
            for j in range(TILE // 128):
                at = slice(j * 128, (j + 1) * 128)
                row = t * (TILE // 128) + j
                part[k, pl.ds(row, n, stride=DEEP), :] = source_real[:, at]
                part[k, pl.ds(PER + row, n, stride=DEEP), :] = source_imag[:, at]

    def flow_copy(d, way, k):
        slot = jnp.where(q + way == d, jnp.where(way > 0, d, chain), d)
        return pltpu.make_async_remote_copy(
            src_ref=flow_out.at[d, k],
            dst_ref=flow_in.at[slot, k],
            send_sem=flow_send.at[d, k],
            recv_sem=flow_recv.at[slot, k],
            device_id={"wide": me + 2 * way},
            device_id_type=MESH,
        )

    def arrival(slot, k):
        return pltpu.make_async_remote_copy(
            src_ref=flow_out.at[0, k],
            dst_ref=flow_in.at[slot, k],
            send_sem=flow_send.at[0, k],
            recv_sem=flow_recv.at[slot, k],
            device_id={"wide": pair},
            device_id_type=MESH,
        )

    pairs = levels // 2
    step_pairs = 6
    loose = (pairs - 1) % step_pairs

    def rounded(value):
        return value.astype(bf16).astype(f32)

    def shape_noise(d, k):
        diag = diagonal(2 * d + h, k)
        root = 0.5 * (diag - jnp.sqrt(jnp.maximum(diag * diag - 4.0, 0.0)))
        once, twice = 2.0 * root, root * root

        def one_pair(i, carry):
            lost, older = carry
            rows = level_rows(2 * i, 2)
            both = part[k, rows, :] + flow_in[d, k, rows, :].astype(f32)
            value = both[:DEEP] + (once * lost - twice * older)
            low = rounded(value)
            lost, older = value - low, lost
            value = both[DEEP:] + (once * lost - twice * older)
            high = rounded(value)
            lost, older = value - high, lost
            flow_out[d, k, rows, :] = jnp.concatenate([low, high], axis=0).astype(bf16)
            return lost, older

        carry = (zeros, zeros)
        for i in range(loose):
            carry = one_pair(i, carry)

        def some_pairs(j, carry):
            for i in range(step_pairs):
                carry = one_pair(loose + j * step_pairs + i, carry)
            return carry

        lost, older = lax.fori_loop(0, (pairs - 1) // step_pairs, some_pairs, carry)
        rows, rest = pl.ds((levels - 2) * DEEP, 2 * DEEP), pl.ds(levels * DEEP, 2 * DEEP)
        both = part[k, rows, :] + flow_in[d, k, rows, :].astype(f32)
        both = both + flow_in[d, k, rest, :].astype(f32)
        both = both + jnp.concatenate([once * lost - twice * older, -(twice * lost)], axis=0)
        kept = rounded(both)
        flow_out[d, k, rows, :] = kept.astype(bf16)
        flow_out[d, k, rest, :] = (both - kept).astype(bf16)

    def pass_on(s, carry):
        d, way = unit(s)
        line_copy(d, 0).wait_recv()
        line_copy(d, 1).wait_recv()
        before = q - way
        for k in range(SECTIONS):
            transform(d, k)

            @pl.when(jnp.logical_and(before >= 0, before < chain))
            def _():
                arrival(d, k).wait_recv()

            shape_noise(d, k)
            flow_copy(d, way, k).start()
        return carry

    lax.fori_loop(0, chain - 1, pass_on, 0)

    line_copy(q, 0).wait_recv()
    line_copy(q, 1).wait_recv()
    for k in range(SECTIONS):
        transform(q, k)

    def end_copy(step, slot, k):
        return pltpu.make_async_remote_copy(
            src_ref=ends.at[slot, k],
            dst_ref=ends.at[slot, k],
            send_sem=end_send.at[step, k],
            recv_sem=end_recv.at[step, k],
            device_id={"lev": (block + step) % lev},
            device_id_type=MESH,
        )

    for k in range(SECTIONS):
        @pl.when(q > 0)
        def _():
            arrival(q, k).wait_recv()

        @pl.when(q < chain - 1)
        def _():
            arrival(chain, k).wait_recv()

        for rest_at, rows_at in ((levels * DEEP, (levels - 2) * DEEP),):
            rows, rest = pl.ds(rows_at, 2 * DEEP), pl.ds(rest_at, 2 * DEEP)
            part[k, rows, :] = part[k, rows, :] + (
                flow_in[q, k, rest, :].astype(f32) + flow_in[chain, k, rest, :].astype(f32)
            )

        def down_pair(i, carry):
            value, first = carry
            rows = level_rows(2 * i, 2)
            both = part[k, rows, :] + (
                flow_in[q, k, rows, :].astype(f32) + flow_in[chain, k, rows, :].astype(f32)
            )
            weighted = from_lo[k, rows, :] * both
            first = first + (weighted[:DEEP] + weighted[DEEP:])
            inverse = coef[k, rows, :]
            low = (both[:DEEP] + value) * inverse[:DEEP]
            high = (both[DEEP:] + low) * inverse[DEEP:]
            part[k, rows, :] = jnp.concatenate([low, high], axis=0)
            return high, first

        value, first = lax.fori_loop(0, pairs, down_pair, (zeros, zeros), unroll=8)
        ends[block, k, 0:DEEP, :] = first
        ends[block, k, DEEP:2 * DEEP, :] = value
        for step in range(1, lev):
            end_copy(step, block, k).start()

    for k in range(SECTIONS):
        near = from_lo[k, 0:DEEP, :]
        distant = from_lo[k, (levels - 1) * DEEP:levels * DEEP, :]
        ratio = near
        ratios, inverses, leads = [ratio], [None], [None]
        for b in range(1, lev):
            inverse = 1.0 / (1.0 - near * ratio)
            lead = distant * ratio * inverse
            ratio = near + lead * distant
            ratios.append(ratio)
            inverses.append(inverse)
            leads.append(lead)
        for step in range(1, lev):
            end_copy(step, (block + lev - step) % lev, k).wait_recv()
        value = ends[0, k, DEEP:2 * DEEP, :]
        values = [value]
        for b in range(1, lev):
            first = ends[b, k, 0:DEEP, :] + near * value
            value = ends[b, k, DEEP:2 * DEEP, :] + distant * value + leads[b] * first
            values.append(value)
        follow = zeros
        first_val[lev] = follow
        last_val[0] = follow
        for b in range(lev - 1, 0, -1):
            follow = inverses[b] * (
                ends[b, k, 0:DEEP, :] + near * values[b - 1] + distant * follow
            )
            first_val[b] = follow
            last_val[b] = values[b - 1] + ratios[b - 1] * follow
        below = last_val[block]

        def up_step(j, carry):
            rows = level_rows(levels - 1 - j)
            carry = part[k, rows, :] + coef[k, rows, :] * carry
            part[k, rows, :] = carry + from_lo[k, rows, :] * below
            return carry

        lax.fori_loop(0, levels, up_step, first_val[block + 1], unroll=8)
        tiles = KXM // 128
        for c in range(2):
            for j in range(PER):
                out_ref[pl.ds(c * levels * tiles + k * PER + j, levels, stride=tiles), :] = part[
                    k, pl.ds(c * PER + j, levels, stride=DEEP), :
                ]

    to_prev.wait_send()
    to_next.wait_send()

    def lines_sent(d, carry):
        line_copy(d, 0).wait_send()
        line_copy(d, 1).wait_send()
        return carry

    lax.fori_loop(0, chain, lines_sent, 0)

    def flows_sent(s, carry):
        d, way = unit(s)
        for k in range(SECTIONS):
            flow_copy(d, way, k).wait_send()
        return carry

    lax.fori_loop(0, chain - 1, flows_sent, 0)
    for k in range(SECTIONS):
        for step in range(1, lev):
            end_copy(step, block, k).wait_send()


def hand_over(x_ref, out_ref):
    out_ref[...] = x_ref[...]


def solution(mesh):
    wide, lev = mesh.shape["wide"], mesh.shape["lev"]
    tables = make_tables()

    def local(nonlinear):
        _, _, levels, rows_ky, chunk = nonlinear.shape
        rows = levels * rows_ky
        halo_rows = max(16, rows_ky)
        chain = wide // 2
        f32, bf16 = jnp.float32, jnp.bfloat16
        dma = pltpu.SemaphoreType.DMA
        pressure = pl.pallas_call(
            functools.partial(kernel, wide, lev, rows_ky, levels),
            out_shape=jax.ShapeDtypeStruct((2 * levels * KXM // 128, 128), f32),
            in_specs=[
                pl.BlockSpec(memory_space=pltpu.VMEM),
                pl.BlockSpec(memory_space=pl.ANY),
            ],
            out_specs=pl.BlockSpec(memory_space=pltpu.VMEM),
            scratch_shapes=[
                pltpu.VMEM((2 * chunk, 2 * KXM), bf16),
                pltpu.VMEM((rows_ky, 4 * levels, chunk), bf16),
                pltpu.VMEM((chain, 4 * levels, chunk), bf16),
                pltpu.VMEM((2, halo_rows, chunk), bf16),
                pltpu.VMEM((2, halo_rows, chunk), bf16),
                pltpu.VMEM((2, rows + 2 * rows_ky, chunk), f32),
                pltpu.VMEM((SECTIONS, levels * DEEP, 128), f32),
                pltpu.VMEM((chain, SECTIONS, (levels + 2) * DEEP, 128), bf16),
                pltpu.VMEM((chain + 1, SECTIONS, (levels + 2) * DEEP, 128), bf16),
                pltpu.VMEM((SECTIONS, levels * DEEP, 128), f32),
                pltpu.VMEM((SECTIONS, levels * DEEP, 128), f32),
                pltpu.VMEM((lev, SECTIONS, 2 * DEEP, 128), f32),
                pltpu.VMEM((lev + 1, DEEP, 128), f32),
                pltpu.VMEM((lev + 1, DEEP, 128), f32),
                dma((2, 4)),
                dma((2,)),
                dma((2,)),
                dma((2, chain)),
                dma((2, chain)),
                dma((chain, SECTIONS)),
                dma((chain + 1, SECTIONS)),
                dma((lev, SECTIONS)),
                dma((lev, SECTIONS)),
            ],
            compiler_params=pltpu.CompilerParams(
                collective_id=0, has_side_effects=True, vmem_limit_bytes=56 * 2**20
            ),
            cost_estimate=pl.CostEstimate(
                flops=2 * 4 * levels * NXG * 2 * KXM,
                bytes_accessed=2 * chunk * 2 * KXM * 2 + 4 * rows * chunk * 2,
                transcendentals=0,
            ),
        )(nonlinear.reshape(3, 2, rows, chunk), jnp.asarray(tables))
        pressure = pl.pallas_call(
            hand_over, out_shape=jax.ShapeDtypeStruct(pressure.shape, f32)
        )(pressure)
        return pressure.reshape(2, levels, 1, KXM)

    placed = (P(None, None, "lev", None, "wide"),)
    return jax.shard_map(
        local, mesh=mesh, in_specs=placed, out_specs=P(None, "lev", "wide", None), check_vma=False
    )
```

```python
import functools
import math

import jax
import jax.numpy as jnp
import ml_dtypes
import numpy as np
from jax import lax
from jax.experimental import pallas as pl
from jax.experimental.pallas import tpu as pltpu
from jax.sharding import PartitionSpec as P

NXG = 4096
KXM = 1536
MESH = pl.DeviceIdType.MESH
SEC = 512
TILE = 256
SECTIONS = KXM // SEC
PER = SEC // 128
DEEP = 2 * PER


def make_tables():
    places = np.arange(NXG, dtype=np.int32)
    waves = np.arange(KXM, dtype=np.int32) - KXM // 2
    phases = np.mod(places[:, None] * waves[None, :], NXG)
    turn = np.arange(NXG, dtype=np.float32) * np.float32(2.0 * math.pi / NXG)
    cosine = np.cos(turn).astype(ml_dtypes.bfloat16)[phases]
    sine = np.sin(turn).astype(ml_dtypes.bfloat16)[phases]
    return np.concatenate([cosine, sine], axis=1)


def level_rows(i, count=1):
    return pl.ds(pl.multiple_of(i * DEEP, DEEP), count * DEEP)


def kernel(
    wide, lev, rows_ky, levels,
    x_ref, tab_ref, out_ref,
    x_buf, tab, send, recv, halo_lo, halo_hi, zpad, part, flow_out, flow_in, coef, from_lo,
    ends, last_val, first_val, lost_val,
    x_sem, tab_sem, halo_send, halo_recv, send_sem, recv_sem, flow_send, flow_recv, end_send, end_recv,
):
    f32, bf16 = jnp.float32, jnp.bfloat16
    chunk = x_ref.shape[3]
    line_rows = levels * rows_ky
    half_levels = levels // 2
    group_levels = max(16, 256 // rows_ky)
    group_rows = group_levels * rows_ky
    groups = levels // group_levels
    halo_rows = halo_lo.shape[1]
    spacing = 2.0 * math.pi / NXG
    me = lax.axis_index("wide")
    block = lax.axis_index("lev")
    chain = wide // 2
    q, h = me // 2, me % 2
    pair = me + 1 - 2 * h

    tab_parts = tab_sem.shape[1]
    tab_rows = chunk // tab_parts

    def tab_copy(side, i):
        owner = me if side == 0 else pair
        at = pl.multiple_of(owner * chunk + i * tab_rows, tab_rows)
        return pltpu.make_async_copy(
            tab_ref.at[pl.ds(at, tab_rows)],
            tab.at[pl.ds(side * chunk + i * tab_rows, tab_rows)],
            tab_sem.at[side, i],
        )

    barrier = pltpu.get_barrier_semaphore()
    pl.semaphore_signal(barrier, inc=1, device_id={"wide": pair}, device_id_type=MESH)

    @pl.when(q > 0)
    def _():
        pl.semaphore_signal(barrier, inc=1, device_id={"wide": me - 2}, device_id_type=MESH)

    @pl.when(q < chain - 1)
    def _():
        pl.semaphore_signal(barrier, inc=1, device_id={"wide": me + 2}, device_id_type=MESH)

    for step in range(1, lev):
        pl.semaphore_signal(
            barrier, inc=1, device_id={"lev": (block + step) % lev}, device_id_type=MESH
        )
    def x_copy(term, c):
        return pltpu.make_async_copy(x_ref.at[term, c], x_buf.at[term, c], x_sem.at[term, c])

    for term in (0, 2, 1):
        for c in range(2):
            x_copy(term, c).start()
    for side in range(2):
        for i in range(tab_parts):
            tab_copy(side, i).start()

    out_row = lax.broadcasted_iota(jnp.int32, (group_rows, group_rows), 0)
    in_row = lax.broadcasted_iota(jnp.int32, (group_rows, group_rows), 1)
    wanted = (out_row % group_levels) * rows_ky + out_row // group_levels
    shuffle = jnp.where(in_row == wanted, 1.0, 0.0).astype(bf16)

    def place(values, c, g):
        moved = jnp.dot(shuffle, values, preferred_element_type=f32).astype(bf16)
        for ky in range(rows_ky):
            send[ky, c, g * group_levels:(g + 1) * group_levels, :] = moved[
                ky * group_levels:(ky + 1) * group_levels
            ]

    upper_far = 1 - (2 * q) // chain
    far = upper_far * (chain - 1 - q) + (1 - upper_far) * q
    near_count = chain - 1 - far
    alone = far - near_count

    def unit(s):
        late = (s - alone + chain) // chain
        t = late * (s - alone)
        distance = (1 - late) * (far - s) + late * (near_count - t // 2)
        up = (1 - late) * upper_far + late * ((1 - upper_far) * (1 - t % 2) + upper_far * (t % 2))
        way = 2 * up - 1
        return q + way * distance, way

    def line_copy(d, which, g):
        rows = (pl.ds(2 * which, 2), pl.ds(g * half_levels, half_levels))
        return pltpu.make_async_remote_copy(
            src_ref=send.at[(2 * d + 1 - h,) + rows],
            dst_ref=recv.at[(d,) + rows],
            send_sem=send_sem.at[which, g, d],
            recv_sem=recv_sem.at[which, g, d],
            device_id={"wide": pair},
            device_id_type=MESH,
        )

    has_prev = (q + chain - 1) // chain
    has_next = (2 * chain - 2 - q) // chain
    pl.semaphore_wait(barrier, lev + has_prev + has_next)
    to_prev = pltpu.make_async_remote_copy(
        src_ref=x_ref.at[2, :, 0:halo_rows],
        dst_ref=halo_hi,
        send_sem=halo_send.at[0],
        recv_sem=halo_recv.at[0],
        device_id={"lev": (block + lev - 1) % lev},
        device_id_type=MESH,
    )
    to_next = pltpu.make_async_remote_copy(
        src_ref=x_ref.at[2, :, line_rows - halo_rows:line_rows],
        dst_ref=halo_lo,
        send_sem=halo_send.at[1],
        recv_sem=halo_recv.at[1],
        device_id={"lev": (block + 1) % lev},
        device_id_type=MESH,
    )
    to_next.start()
    to_prev.start()
    first_unit, first_way = unit(0)
    for c in range(2):
        x_copy(0, c).wait()
    for part_of in range(2):
        for g in range(part_of * groups // 2, (part_of + 1) * groups // 2):
            for c in range(2):
                place(x_buf[0, c, g * group_rows:(g + 1) * group_rows, :], c, g)
        if part_of == 0:
            line_copy(first_unit, 0, 0).start()

    for c in range(2):
        x_copy(2, c).wait()
        zpad[c, rows_ky:rows_ky + line_rows, :] = x_buf[2, c].astype(f32)
    for c in range(2):
        x_copy(1, c).wait()
    ky_row = lax.broadcasted_iota(jnp.int32, (group_rows, chunk), 0) % rows_ky
    ky_scaled = ky_row.astype(f32) * spacing
    for part_of in range(2):
        if part_of == 0:
            to_next.wait_recv()
            for c in range(2):
                low = halo_lo[c].astype(f32)[halo_rows - rows_ky:]
                zpad[c, 0:rows_ky, :] = jnp.where(block > 0, low, 0.0)
        else:
            to_prev.wait_recv()
            for c in range(2):
                high = halo_hi[c].astype(f32)[:rows_ky]
                zpad[c, rows_ky + line_rows:, :] = jnp.where(block < lev - 1, high, 0.0)
        for g in range(part_of * groups // 2, (part_of + 1) * groups // 2):
            for c in range(2):
                at = g * group_rows
                upper = zpad[c, at + 2 * rows_ky:at + 2 * rows_ky + group_rows, :]
                lower = zpad[c, at:at + group_rows, :]
                turned = ky_scaled * x_buf[1, 1 - c, at:at + group_rows, :].astype(f32)
                slope = (upper - lower) * 0.5
                mixed = slope - turned if c == 0 else slope + turned
                place(mixed.astype(bf16), 2 + c, g)
        line_copy(first_unit, 1, part_of).start()
        if part_of == 0:
            line_copy(first_unit, 0, 1).start()

    def send_lines(s, carry):
        d, _ = unit(s)
        for which in range(2):
            for g in range(2):
                line_copy(d, which, g).start()
        return carry

    lax.fori_loop(1, chain, send_lines, 0)

    def clear(slot):
        for k in range(SECTIONS):
            flow_in[slot, k] = jnp.zeros(flow_in.shape[2:], bf16)

    @pl.when(q == 0)
    def _():
        @pl.loop(0, chain)
        def _(slot):
            clear(slot)

    @pl.when(q == chain - 1)
    def _():
        @pl.loop(0, chain - 1)
        def _(slot):
            clear(slot)

        clear(chain)

    part_row = lax.broadcasted_iota(jnp.int32, (DEEP, 128), 0)
    lane = lax.broadcasted_iota(jnp.int32, (DEEP, 128), 1)

    def diagonal(ky, k):
        column = k * SEC + (part_row % PER) * 128 + lane
        kx = (column - KXM // 2).astype(f32) * spacing
        kyd = ky.astype(f32) * spacing
        return 2.0 + (kyd * kyd + kx * kx)

    own_diagonal = [diagonal(me, k) for k in range(SECTIONS)]

    def coef_step(i, carry):
        after = []
        for k in range(SECTIONS):
            shift, gain = carry[2 * k], carry[2 * k + 1]
            inverse = 1.0 / (own_diagonal[k] - shift)
            gain = gain * inverse
            coef[k, level_rows(i), :] = inverse
            from_lo[k, level_rows(i), :] = gain
            after += [inverse, gain]
        return tuple(after)

    zeros = jnp.zeros((DEEP, 128), f32)
    ones = jnp.ones((DEEP, 128), f32)
    lax.fori_loop(0, levels, coef_step, (zeros, ones) * SECTIONS)

    def unit_step(j, carry):
        i = levels - 1 - j
        after = []
        for k in range(SECTIONS):
            low = from_lo[k, level_rows(i), :] + coef[k, level_rows(i), :] * carry[k]
            from_lo[k, level_rows(i), :] = low
            after.append(low)
        return tuple(after)

    lax.fori_loop(0, levels, unit_step, (zeros,) * SECTIONS)

    for side in range(2):
        for i in range(tab_parts):
            tab_copy(side, i).wait()

    norm_scale = 1.0 / math.sqrt(NXG)

    def transform(d, k, begin, n):
        rows = slice(begin, begin + n)
        lines = jnp.concatenate(
            [
                send[2 * d + h, :, rows, :].reshape(4 * n, chunk),
                recv[d, :, rows, :].reshape(4 * n, chunk),
            ],
            axis=1,
        )
        for t in range(SEC // TILE):
            first = k * SEC + t * TILE
            with_cos = jnp.dot(lines, tab[:, first:first + TILE], preferred_element_type=f32)
            with_sin = jnp.dot(
                lines, tab[:, KXM + first:KXM + first + TILE], preferred_element_type=f32
            )
            kx = (
                lax.broadcasted_iota(jnp.int32, (1, TILE), 1) + first - KXM // 2
            ).astype(f32) * spacing
            fx_real = (with_cos[0:n] + with_sin[n:2 * n]) * norm_scale
            fx_imag = (with_cos[n:2 * n] - with_sin[0:n]) * norm_scale
            fg_real = (with_cos[2 * n:3 * n] + with_sin[3 * n:4 * n]) * norm_scale
            fg_imag = (with_cos[3 * n:4 * n] - with_sin[2 * n:3 * n]) * norm_scale
            source_real = kx * fx_imag - fg_real
            source_imag = -kx * fx_real - fg_imag
            for j in range(TILE // 128):
                at = slice(j * 128, (j + 1) * 128)
                row = begin * DEEP + t * (TILE // 128) + j
                part[k, pl.ds(row, n, stride=DEEP), :] = source_real[:, at]
                part[k, pl.ds(PER + row, n, stride=DEEP), :] = source_imag[:, at]

    flow_rows = (pl.ds(0, half_levels * DEEP), pl.ds(half_levels * DEEP, (half_levels + 2) * DEEP))

    def flow_copy(d, way, k, g):
        slot = jnp.where(q + way == d, jnp.where(way > 0, d, chain), d)
        return pltpu.make_async_remote_copy(
            src_ref=flow_out.at[d, k, flow_rows[g]],
            dst_ref=flow_in.at[slot, k, flow_rows[g]],
            send_sem=flow_send.at[d, k, g],
            recv_sem=flow_recv.at[slot, k, g],
            device_id={"wide": me + 2 * way},
            device_id_type=MESH,
        )

    def arrival(slot, k, g):
        return pltpu.make_async_remote_copy(
            src_ref=flow_out.at[0, k, flow_rows[g]],
            dst_ref=flow_in.at[slot, k, flow_rows[g]],
            send_sem=flow_send.at[0, k, g],
            recv_sem=flow_recv.at[slot, k, g],
            device_id={"wide": pair},
            device_id_type=MESH,
        )

    def over_pairs(body, begin, count, carry):
        group = max(n for n in range(1, 9) if count % n == 0)

        def some(j, carry):
            for i in range(group):
                carry = body(begin + j * group + i, carry)
            return carry

        return lax.fori_loop(0, count // group, some, carry)

    half_pairs = half_levels // 2

    def rounded(value):
        return value.astype(bf16).astype(f32)

    def shape_noise(d, k, g, carry):
        diag = diagonal(2 * d + h, k)
        root = 0.5 * (diag - jnp.sqrt(jnp.maximum(diag * diag - 4.0, 0.0)))
        once, twice = 2.0 * root, root * root

        def one_pair(i, carry):
            lost, older = carry
            rows = level_rows(2 * i, 2)
            both = part[k, rows, :] + flow_in[d, k, rows, :].astype(f32)
            value = both[:DEEP] + (once * lost - twice * older)
            low = rounded(value)
            lost, older = value - low, lost
            value = both[DEEP:] + (once * lost - twice * older)
            high = rounded(value)
            lost, older = value - high, lost
            flow_out[d, k, rows, :] = jnp.concatenate([low, high], axis=0).astype(bf16)
            return lost, older

        if g == 0:
            return over_pairs(one_pair, 0, half_pairs, carry)
        lost, older = over_pairs(one_pair, half_pairs, half_pairs - 1, carry)
        rows, rest = pl.ds((levels - 2) * DEEP, 2 * DEEP), pl.ds(levels * DEEP, 2 * DEEP)
        both = part[k, rows, :] + flow_in[d, k, rows, :].astype(f32)
        both = both + flow_in[d, k, rest, :].astype(f32)
        both = both + jnp.concatenate([once * lost - twice * older, -(twice * lost)], axis=0)
        kept = rounded(both)
        flow_out[d, k, rows, :] = kept.astype(bf16)
        flow_out[d, k, rest, :] = (both - kept).astype(bf16)
        return carry

    def await_flow(d, way, k, g):
        before = q - way

        @pl.when(jnp.logical_and(before >= 0, before < chain))
        def _():
            arrival(d, k, g).wait_recv()

    def await_lines(d, g):
        for which in range(2):
            line_copy(d, which, g).wait_recv()

    for g in range(2):
        await_lines(first_unit, g)
        for k in range(SECTIONS):
            transform(first_unit, k, g * half_levels, half_levels)
            await_flow(first_unit, first_way, k, g)
            if g == 0:
                lost, older = shape_noise(first_unit, k, g, (zeros, zeros))
                lost_val[k, 0] = lost
                lost_val[k, 1] = older
            else:
                shape_noise(first_unit, k, g, (lost_val[k, 0], lost_val[k, 1]))
            flow_copy(first_unit, first_way, k, g).start()

    def pass_on(s, carry):
        d, way = unit(s)
        await_lines(d, 0)
        await_lines(d, 1)
        for k in range(SECTIONS):
            transform(d, k, 0, levels)
            lost = (zeros, zeros)
            for g in range(2):
                await_flow(d, way, k, g)
                lost = shape_noise(d, k, g, lost)
                flow_copy(d, way, k, g).start()
        return carry

    lax.fori_loop(1, chain - 1, pass_on, 0)

    await_lines(q, 0)
    await_lines(q, 1)
    for k in range(SECTIONS):
        transform(q, k, 0, levels)

    def end_copy(step, slot, k):
        return pltpu.make_async_remote_copy(
            src_ref=ends.at[slot, k],
            dst_ref=ends.at[slot, k],
            send_sem=end_send.at[step, k],
            recv_sem=end_recv.at[step, k],
            device_id={"lev": (block + step) % lev},
            device_id_type=MESH,
        )

    def down_pass(k):
        def down_pair(i, carry):
            value, first = carry
            rows = level_rows(2 * i, 2)
            both = part[k, rows, :] + (
                flow_in[q, k, rows, :].astype(f32) + flow_in[chain, k, rows, :].astype(f32)
            )
            weighted = from_lo[k, rows, :] * both
            first = first + (weighted[:DEEP] + weighted[DEEP:])
            inverse = coef[k, rows, :]
            low = (both[:DEEP] + value) * inverse[:DEEP]
            high = (both[DEEP:] + low) * inverse[DEEP:]
            part[k, rows, :] = jnp.concatenate([low, high], axis=0)
            return high, first

        carry = (zeros, zeros)
        for g in range(2):
            @pl.when(q > 0)
            def _():
                arrival(q, k, g).wait_recv()

            @pl.when(q < chain - 1)
            def _():
                arrival(chain, k, g).wait_recv()

            if g == 1:
                rows, rest = pl.ds((levels - 2) * DEEP, 2 * DEEP), pl.ds(levels * DEEP, 2 * DEEP)
                part[k, rows, :] = part[k, rows, :] + (
                    flow_in[q, k, rest, :].astype(f32) + flow_in[chain, k, rest, :].astype(f32)
                )
            carry = over_pairs(down_pair, g * half_pairs, half_pairs, carry)
        value, first = carry
        ends[block, k, 0:DEEP, :] = first
        ends[block, k, DEEP:2 * DEEP, :] = value
        for step in range(1, lev):
            end_copy(step, block, k).start()

    def up_pass(k):
        near = from_lo[k, 0:DEEP, :]
        distant = from_lo[k, (levels - 1) * DEEP:levels * DEEP, :]
        ratio = near
        ratios, inverses, leads = [ratio], [None], [None]
        for b in range(1, lev):
            inverse = 1.0 / (1.0 - near * ratio)
            lead = distant * ratio * inverse
            ratio = near + lead * distant
            ratios.append(ratio)
            inverses.append(inverse)
            leads.append(lead)
        for step in range(1, lev):
            end_copy(step, (block + lev - step) % lev, k).wait_recv()
        value = ends[0, k, DEEP:2 * DEEP, :]
        values = [value]
        for b in range(1, lev):
            first = ends[b, k, 0:DEEP, :] + near * value
            value = ends[b, k, DEEP:2 * DEEP, :] + distant * value + leads[b] * first
            values.append(value)
        follow = zeros
        first_val[lev] = follow
        last_val[0] = follow
        for b in range(lev - 1, 0, -1):
            follow = inverses[b] * (
                ends[b, k, 0:DEEP, :] + near * values[b - 1] + distant * follow
            )
            first_val[b] = follow
            last_val[b] = values[b - 1] + ratios[b - 1] * follow
        below = last_val[block]

        def up_pair(j, carry):
            rows = level_rows(levels - 2 - 2 * j, 2)
            both, inverse = part[k, rows, :], coef[k, rows, :]
            high = both[DEEP:] + inverse[DEEP:] * carry
            low = both[:DEEP] + inverse[:DEEP] * high
            gain = from_lo[k, rows, :]
            part[k, rows, :] = jnp.concatenate(
                [low + gain[:DEEP] * below, high + gain[DEEP:] * below], axis=0
            )
            return low

        over_pairs(up_pair, 0, levels // 2, first_val[block + 1])
        tiles = KXM // 128
        for c in range(2):
            for j in range(PER):
                out_ref[pl.ds(c * levels * tiles + k * PER + j, levels, stride=tiles), :] = part[
                    k, pl.ds(c * PER + j, levels, stride=DEEP), :
                ]

    for k in range(SECTIONS):
        down_pass(k)
        if k > 0 and k < SECTIONS - 1:
            up_pass(k - 1)
    for k in range(max(SECTIONS - 2, 0), SECTIONS):
        up_pass(k)

    to_prev.wait_send()
    to_next.wait_send()

    def lines_sent(d, carry):
        for which in range(2):
            for g in range(2):
                line_copy(d, which, g).wait_send()
        return carry

    lax.fori_loop(0, chain, lines_sent, 0)

    def flows_sent(s, carry):
        d, way = unit(s)
        for k in range(SECTIONS):
            for g in range(2):
                flow_copy(d, way, k, g).wait_send()
        return carry

    lax.fori_loop(0, chain - 1, flows_sent, 0)
    for k in range(SECTIONS):
        for step in range(1, lev):
            end_copy(step, block, k).wait_send()


def solution(mesh):
    wide, lev = mesh.shape["wide"], mesh.shape["lev"]
    tables = make_tables()

    def local(nonlinear):
        _, _, levels, rows_ky, chunk = nonlinear.shape
        rows = levels * rows_ky
        halo_rows = max(16, rows_ky)
        chain = wide // 2
        f32, bf16 = jnp.float32, jnp.bfloat16
        dma = pltpu.SemaphoreType.DMA
        pressure = pl.pallas_call(
            functools.partial(kernel, wide, lev, rows_ky, levels),
            out_shape=pltpu.VMEM((2 * levels * KXM // 128, 128), f32),
            in_specs=[
                pl.BlockSpec(memory_space=pl.ANY),
                pl.BlockSpec(memory_space=pl.ANY),
            ],
            out_specs=pl.BlockSpec(memory_space=pltpu.VMEM),
            scratch_shapes=[
                pltpu.VMEM((3, 2, rows, chunk), bf16),
                pltpu.VMEM((2 * chunk, 2 * KXM), bf16),
                pltpu.VMEM((rows_ky, 4, levels, chunk), bf16),
                pltpu.VMEM((chain, 4, levels, chunk), bf16),
                pltpu.VMEM((2, halo_rows, chunk), bf16),
                pltpu.VMEM((2, halo_rows, chunk), bf16),
                pltpu.VMEM((2, rows + 2 * rows_ky, chunk), f32),
                pltpu.VMEM((SECTIONS, levels * DEEP, 128), f32),
                pltpu.VMEM((chain, SECTIONS, (levels + 2) * DEEP, 128), bf16),
                pltpu.VMEM((chain + 1, SECTIONS, (levels + 2) * DEEP, 128), bf16),
                pltpu.VMEM((SECTIONS, levels * DEEP, 128), f32),
                pltpu.VMEM((SECTIONS, levels * DEEP, 128), f32),
                pltpu.VMEM((lev, SECTIONS, 2 * DEEP, 128), f32),
                pltpu.VMEM((lev + 1, DEEP, 128), f32),
                pltpu.VMEM((lev + 1, DEEP, 128), f32),
                pltpu.VMEM((SECTIONS, 2, DEEP, 128), f32),
                dma((3, 2)),
                dma((2, 4)),
                dma((2,)),
                dma((2,)),
                dma((2, 2, chain)),
                dma((2, 2, chain)),
                dma((chain, SECTIONS, 2)),
                dma((chain + 1, SECTIONS, 2)),
                dma((lev, SECTIONS)),
                dma((lev, SECTIONS)),
            ],
            compiler_params=pltpu.CompilerParams(
                collective_id=0, has_side_effects=True, vmem_limit_bytes=56 * 2**20
            ),
            cost_estimate=pl.CostEstimate(
                flops=2 * 4 * levels * NXG * 2 * KXM,
                bytes_accessed=2 * chunk * 2 * KXM * 2 + 4 * rows * chunk * 2,
                transcendentals=0,
            ),
        )(nonlinear.reshape(3, 2, rows, chunk), jnp.asarray(tables))
        return pressure.reshape(2, levels, 1, KXM)

    placed = (P(None, None, "lev", None, "wide"),)
    return jax.shard_map(
        local, mesh=mesh, in_specs=placed, out_specs=P(None, "lev", "wide", None), check_vma=False
    )
```

```python
import functools
import math

import jax
import jax.numpy as jnp
import ml_dtypes
import numpy as np
from jax import lax
from jax.experimental import pallas as pl
from jax.experimental.pallas import tpu as pltpu
from jax.sharding import PartitionSpec as P

NXG = 4096
KXM = 1536
MESH = pl.DeviceIdType.MESH
SEC = 512
TILE = 256
SECTIONS = KXM // SEC
PER = SEC // 128
DEEP = 2 * PER


def make_tables():
    places = np.arange(NXG, dtype=np.int32)
    waves = np.arange(KXM, dtype=np.int32) - KXM // 2
    phases = np.mod(places[:, None] * waves[None, :], NXG)
    turn = np.arange(NXG, dtype=np.float32) * np.float32(2.0 * math.pi / NXG)
    cosine = np.cos(turn).astype(ml_dtypes.bfloat16)[phases]
    sine = np.sin(turn).astype(ml_dtypes.bfloat16)[phases]
    return np.concatenate([cosine, sine], axis=1)


def level_rows(i, count=1):
    return pl.ds(pl.multiple_of(i * DEEP, DEEP), count * DEEP)


def kernel(
    wide, lev, rows_ky, levels,
    x_ref, tab_ref, out_ref,
    x_buf, tab, send, recv, halo_lo, halo_hi, zpad, part, own_part, flow_out, flow_in, coef, from_lo,
    ends, last_val, first_val, lost_val,
    x_sem, tab_sem, halo_send, halo_recv, send_sem, recv_sem, flow_send, flow_recv, end_send, end_recv,
):
    f32, bf16 = jnp.float32, jnp.bfloat16
    chunk = x_ref.shape[3]
    line_rows = levels * rows_ky
    half_levels = levels // 2
    group_levels = max(16, 256 // rows_ky)
    group_rows = group_levels * rows_ky
    groups = levels // group_levels
    halo_rows = halo_lo.shape[1]
    spacing = 2.0 * math.pi / NXG
    me = lax.axis_index("wide")
    block = lax.axis_index("lev")
    chain = wide // 2
    q, h = me // 2, me % 2
    pair = me + 1 - 2 * h
    has_prev = (q + chain - 1) // chain
    has_next = (2 * chain - 2 - q) // chain

    tab_parts = tab_sem.shape[1]
    tab_rows = chunk // tab_parts

    def tab_copy(side, i):
        at = pl.multiple_of((me if side == 0 else pair) * chunk + i * tab_rows, tab_rows)
        return pltpu.make_async_copy(
            tab_ref.at[pl.ds(at, tab_rows)],
            tab.at[pl.ds(side * chunk + i * tab_rows, tab_rows)],
            tab_sem.at[side, i],
        )

    barrier = pltpu.get_barrier_semaphore()
    pl.semaphore_signal(barrier, inc=1, device_id={"wide": pair}, device_id_type=MESH)

    @pl.when(q > 0)
    def _():
        pl.semaphore_signal(barrier, inc=1, device_id={"wide": me - 2}, device_id_type=MESH)

    @pl.when(q < chain - 1)
    def _():
        pl.semaphore_signal(barrier, inc=1, device_id={"wide": me + 2}, device_id_type=MESH)

    for step in range(1, lev):
        pl.semaphore_signal(
            barrier, inc=1, device_id={"lev": (block + step) % lev}, device_id_type=MESH
        )
    def x_copy(term, c):
        return pltpu.make_async_copy(x_ref.at[term, c], x_buf.at[term, c], x_sem.at[term, c])

    for term in (0, 2, 1):
        for c in range(2):
            x_copy(term, c).start()
    out_row = lax.broadcasted_iota(jnp.int32, (group_rows, group_rows), 0)
    in_row = lax.broadcasted_iota(jnp.int32, (group_rows, group_rows), 1)
    wanted = (out_row % group_levels) * rows_ky + out_row // group_levels
    shuffle = jnp.where(in_row == wanted, 1.0, 0.0).astype(bf16)

    def place(values, c, g):
        moved = jnp.dot(shuffle, values, preferred_element_type=f32).astype(bf16)
        for ky in range(rows_ky):
            send[ky, c, g * group_levels:(g + 1) * group_levels, :] = moved[
                ky * group_levels:(ky + 1) * group_levels
            ]

    upper_far = 1 - (2 * q) // chain
    far = upper_far * (chain - 1 - q) + (1 - upper_far) * q
    near_count = chain - 1 - far
    alone = far - near_count

    def unit(s):
        late = (s - alone + chain) // chain
        t = late * (s - alone)
        distance = (1 - late) * (far - s) + late * (near_count - t // 2)
        up = (1 - late) * upper_far + late * ((1 - upper_far) * (1 - t % 2) + upper_far * (t % 2))
        way = 2 * up - 1
        return q + way * distance, way

    def line_copy(d, which, g):
        rows = (pl.ds(2 * which, 2), pl.ds(g * half_levels, half_levels))
        return pltpu.make_async_remote_copy(
            src_ref=send.at[(2 * d + 1 - h,) + rows],
            dst_ref=recv.at[(d,) + rows],
            send_sem=send_sem.at[which, g, d],
            recv_sem=recv_sem.at[which, g, d],
            device_id={"wide": pair},
            device_id_type=MESH,
        )

    pl.semaphore_wait(barrier, lev + has_prev + has_next)
    to_prev = pltpu.make_async_remote_copy(
        src_ref=x_ref.at[2, :, 0:halo_rows],
        dst_ref=halo_hi,
        send_sem=halo_send.at[0],
        recv_sem=halo_recv.at[0],
        device_id={"lev": (block + lev - 1) % lev},
        device_id_type=MESH,
    )
    to_next = pltpu.make_async_remote_copy(
        src_ref=x_ref.at[2, :, line_rows - halo_rows:line_rows],
        dst_ref=halo_lo,
        send_sem=halo_send.at[1],
        recv_sem=halo_recv.at[1],
        device_id={"lev": (block + 1) % lev},
        device_id_type=MESH,
    )
    to_next.start()
    to_prev.start()

    first_unit, first_way = unit(0)
    for c in range(2):
        x_copy(0, c).wait()
    for part_of in range(2):
        for g in range(part_of * groups // 2, (part_of + 1) * groups // 2):
            for c in range(2):
                place(x_buf[0, c, g * group_rows:(g + 1) * group_rows, :], c, g)
        if part_of == 0:
            line_copy(first_unit, 0, 0).start()

    for c in range(2):
        x_copy(2, c).wait()
        zpad[c, rows_ky:rows_ky + line_rows, :] = x_buf[2, c].astype(f32)
    for c in range(2):
        x_copy(1, c).wait()
    for side in range(2):
        for i in range(tab_parts):
            tab_copy(side, i).start()
    ky_row = lax.broadcasted_iota(jnp.int32, (group_rows, chunk), 0) % rows_ky
    ky_scaled = ky_row.astype(f32) * spacing
    for part_of in range(2):
        if part_of == 0:
            to_next.wait_recv()
            for c in range(2):
                low = halo_lo[c].astype(f32)[halo_rows - rows_ky:]
                zpad[c, 0:rows_ky, :] = jnp.where(block > 0, low, 0.0)
        else:
            to_prev.wait_recv()
            for c in range(2):
                high = halo_hi[c].astype(f32)[:rows_ky]
                zpad[c, rows_ky + line_rows:, :] = jnp.where(block < lev - 1, high, 0.0)
        for g in range(part_of * groups // 2, (part_of + 1) * groups // 2):
            for c in range(2):
                at = g * group_rows
                upper = zpad[c, at + 2 * rows_ky:at + 2 * rows_ky + group_rows, :]
                lower = zpad[c, at:at + group_rows, :]
                turned = ky_scaled * x_buf[1, 1 - c, at:at + group_rows, :].astype(f32)
                slope = (upper - lower) * 0.5
                mixed = slope - turned if c == 0 else slope + turned
                place(mixed.astype(bf16), 2 + c, g)
        line_copy(first_unit, 1, part_of).start()
        if part_of == 0:
            line_copy(first_unit, 0, 1).start()

    def start_lines(d):
        for which in range(2):
            for g in range(2):
                line_copy(d, which, g).start()

    def send_lines(s, carry):
        d, _ = unit(s)
        start_lines(d)
        return carry

    lax.fori_loop(1, chain, send_lines, 0)

    def clear(slot):
        for k in range(SECTIONS):
            flow_in[slot, k] = jnp.zeros(flow_in.shape[2:], bf16)

    @pl.when(q == 0)
    def _():
        @pl.loop(0, chain)
        def _(slot):
            clear(slot)

    @pl.when(q == chain - 1)
    def _():
        @pl.loop(0, chain - 1)
        def _(slot):
            clear(slot)

        clear(chain)

    part_row = lax.broadcasted_iota(jnp.int32, (DEEP, 128), 0)
    lane = lax.broadcasted_iota(jnp.int32, (DEEP, 128), 1)

    def diagonal(ky, k):
        column = k * SEC + (part_row % PER) * 128 + lane
        kx = (column - KXM // 2).astype(f32) * spacing
        kyd = ky.astype(f32) * spacing
        return 2.0 + (kyd * kyd + kx * kx)

    own_diagonal = [diagonal(me, k) for k in range(SECTIONS)]

    def coef_step(i, carry):
        after = []
        for k in range(SECTIONS):
            shift, gain = carry[2 * k], carry[2 * k + 1]
            inverse = 1.0 / (own_diagonal[k] - shift)
            gain = gain * inverse
            coef[k, level_rows(i), :] = inverse
            from_lo[k, level_rows(i), :] = gain
            after += [inverse, gain]
        return tuple(after)

    zeros = jnp.zeros((DEEP, 128), f32)
    ones = jnp.ones((DEEP, 128), f32)
    lax.fori_loop(0, levels, coef_step, (zeros, ones) * SECTIONS)

    def unit_step(j, carry):
        i = levels - 1 - j
        after = []
        for k in range(SECTIONS):
            low = from_lo[k, level_rows(i), :] + coef[k, level_rows(i), :] * carry[k]
            from_lo[k, level_rows(i), :] = low
            after.append(low)
        return tuple(after)

    lax.fori_loop(0, levels, unit_step, (zeros,) * SECTIONS)

    for side in range(2):
        for i in range(tab_parts):
            tab_copy(side, i).wait()

    norm_scale = 1.0 / math.sqrt(NXG)

    def transform(target, k, begin, n, holders, table):
        rows = slice(begin, begin + n)
        lines = jnp.concatenate(
            [holder[:, rows, :].reshape(4 * n, chunk) for holder in holders], axis=1
        )
        for t in range(SEC // TILE):
            first = k * SEC + t * TILE
            cos_at, sin_at = pl.multiple_of(first, TILE), pl.multiple_of(KXM + first, TILE)
            with_cos = jnp.dot(
                lines, table[:, pl.ds(cos_at, TILE)], preferred_element_type=f32
            )
            with_sin = jnp.dot(
                lines, table[:, pl.ds(sin_at, TILE)], preferred_element_type=f32
            )
            kx = (
                lax.broadcasted_iota(jnp.int32, (1, TILE), 1) + first - KXM // 2
            ).astype(f32) * spacing
            fx_real = (with_cos[0:n] + with_sin[n:2 * n]) * norm_scale
            fx_imag = (with_cos[n:2 * n] - with_sin[0:n]) * norm_scale
            fg_real = (with_cos[2 * n:3 * n] + with_sin[3 * n:4 * n]) * norm_scale
            fg_imag = (with_cos[3 * n:4 * n] - with_sin[2 * n:3 * n]) * norm_scale
            source_real = kx * fx_imag - fg_real
            source_imag = -kx * fx_real - fg_imag
            for j in range(TILE // 128):
                at = slice(j * 128, (j + 1) * 128)
                place_at = begin * DEEP + t * (TILE // 128) + j
                for c, source in ((0, source_real), (1, source_imag)):
                    where = pl.ds(c * PER + place_at, n, stride=DEEP)
                    target[k, where, :] = source[:, at]

    def transform_unit(d, k, begin, n):
        transform(part, k, begin, n, [send.at[2 * d + h], recv.at[d]], tab)

    flow_rows = (pl.ds(0, half_levels * DEEP), pl.ds(half_levels * DEEP, (half_levels + 2) * DEEP))

    def flow_copy(d, way, k, g):
        slot = jnp.where(q + way == d, jnp.where(way > 0, d, chain), d)
        return pltpu.make_async_remote_copy(
            src_ref=flow_out.at[d, k, flow_rows[g]],
            dst_ref=flow_in.at[slot, k, flow_rows[g]],
            send_sem=flow_send.at[d, k, g],
            recv_sem=flow_recv.at[slot, k, g],
            device_id={"wide": me + 2 * way},
            device_id_type=MESH,
        )

    def arrival(slot, k, g):
        return pltpu.make_async_remote_copy(
            src_ref=flow_out.at[0, k, flow_rows[g]],
            dst_ref=flow_in.at[slot, k, flow_rows[g]],
            send_sem=flow_send.at[0, k, g],
            recv_sem=flow_recv.at[slot, k, g],
            device_id={"wide": pair},
            device_id_type=MESH,
        )

    def over_pairs(body, begin, count, carry):
        group = max(n for n in range(1, 9) if count % n == 0)

        def some(j, carry):
            for i in range(group):
                carry = body(begin + j * group + i, carry)
            return carry

        return lax.fori_loop(0, count // group, some, carry)

    half_pairs = half_levels // 2

    def rounded(value):
        return value.astype(bf16).astype(f32)

    def shape_noise(d, k, g, carry):
        diag = diagonal(2 * d + h, k)
        root = 0.5 * (diag - jnp.sqrt(jnp.maximum(diag * diag - 4.0, 0.0)))
        once, twice = 2.0 * root, root * root

        def one_pair(i, carry):
            lost, older = carry
            rows = level_rows(2 * i, 2)
            both = part[k, rows, :] + flow_in[d, k, rows, :].astype(f32)
            value = both[:DEEP] + (once * lost - twice * older)
            low = rounded(value)
            lost, older = value - low, lost
            value = both[DEEP:] + (once * lost - twice * older)
            high = rounded(value)
            lost, older = value - high, lost
            flow_out[d, k, rows, :] = jnp.concatenate([low, high], axis=0).astype(bf16)
            return lost, older

        if g == 0:
            return over_pairs(one_pair, 0, half_pairs, carry)
        lost, older = over_pairs(one_pair, half_pairs, half_pairs - 1, carry)
        rows, rest = pl.ds((levels - 2) * DEEP, 2 * DEEP), pl.ds(levels * DEEP, 2 * DEEP)
        both = part[k, rows, :] + flow_in[d, k, rows, :].astype(f32)
        both = both + flow_in[d, k, rest, :].astype(f32)
        both = both + jnp.concatenate([once * lost - twice * older, -(twice * lost)], axis=0)
        kept = rounded(both)
        flow_out[d, k, rows, :] = kept.astype(bf16)
        flow_out[d, k, rest, :] = (both - kept).astype(bf16)
        return carry

    def await_flow(d, way, k, g):
        before = q - way

        @pl.when(jnp.logical_and(before >= 0, before < chain))
        def _():
            arrival(d, k, g).wait_recv()

    def await_lines(d, g):
        for which in range(2):
            line_copy(d, which, g).wait_recv()

    for g in range(2):
        await_lines(first_unit, g)
        for k in range(SECTIONS):
            transform_unit(first_unit, k, g * half_levels, half_levels)
            await_flow(first_unit, first_way, k, g)
            if g == 0:
                lost, older = shape_noise(first_unit, k, g, (zeros, zeros))
                lost_val[k, 0] = lost
                lost_val[k, 1] = older
            else:
                shape_noise(first_unit, k, g, (lost_val[k, 0], lost_val[k, 1]))
            flow_copy(first_unit, first_way, k, g).start()

    def pass_unit(d, way):
        for k in range(SECTIONS):
            transform_unit(d, k, 0, levels)
            lost = (zeros, zeros)
            for g in range(2):
                await_flow(d, way, k, g)
                lost = shape_noise(d, k, g, lost)
                flow_copy(d, way, k, g).start()

    def pass_on(s, carry):
        d, way = unit(s)
        await_lines(d, 0)
        await_lines(d, 1)
        pass_unit(d, way)
        return carry

    lax.fori_loop(1, chain - 1, pass_on, 0)
    await_lines(q, 0)
    await_lines(q, 1)

    @pl.loop(0, SECTIONS)
    def _(k):
        transform(own_part, k, 0, levels, [send.at[me], recv.at[q]], tab)

    section_groups = (range(SECTIONS - 1), range(SECTIONS - 1, SECTIONS))

    def end_copy(step, slot, n):
        sections = pl.ds(section_groups[n][0], len(section_groups[n]))
        return pltpu.make_async_remote_copy(
            src_ref=ends.at[slot, sections],
            dst_ref=ends.at[slot, sections],
            send_sem=end_send.at[step, n],
            recv_sem=end_recv.at[step, n],
            device_id={"lev": (block + step) % lev},
            device_id_type=MESH,
        )

    def down_pass(n):
        sections = section_groups[n]

        def down_pair(i, carry):
            rows = level_rows(2 * i, 2)
            after = []
            for i_k, k in enumerate(sections):
                value, first = carry[2 * i_k], carry[2 * i_k + 1]
                both = own_part[k, rows, :] + (
                    flow_in[q, k, rows, :].astype(f32) + flow_in[chain, k, rows, :].astype(f32)
                )
                weighted = from_lo[k, rows, :] * both
                first = first + (weighted[:DEEP] + weighted[DEEP:])
                inverse = coef[k, rows, :]
                low = (both[:DEEP] + value) * inverse[:DEEP]
                high = (both[DEEP:] + low) * inverse[DEEP:]
                own_part[k, rows, :] = jnp.concatenate([low, high], axis=0)
                after += [high, first]
            return tuple(after)

        carry = (zeros, zeros) * len(sections)
        for g in range(2):
            for k in sections:
                @pl.when(q > 0)
                def _():
                    arrival(q, k, g).wait_recv()

                @pl.when(q < chain - 1)
                def _():
                    arrival(chain, k, g).wait_recv()

                if g == 1:
                    rows = pl.ds((levels - 2) * DEEP, 2 * DEEP)
                    rest = pl.ds(levels * DEEP, 2 * DEEP)
                    own_part[k, rows, :] = own_part[k, rows, :] + (
                        flow_in[q, k, rest, :].astype(f32)
                        + flow_in[chain, k, rest, :].astype(f32)
                    )
            carry = over_pairs(down_pair, g * half_pairs, half_pairs, carry)
        for i_k, k in enumerate(sections):
            ends[block, k, 0:DEEP, :] = carry[2 * i_k + 1]
            ends[block, k, DEEP:2 * DEEP, :] = carry[2 * i_k]
        for step in range(1, lev):
            end_copy(step, block, n).start()

    def up_pass(n):
        sections = section_groups[n]
        nears, distants, ratios, inverses, leads = [], [], [], [], []
        for k in sections:
            near = from_lo[k, 0:DEEP, :]
            distant = from_lo[k, (levels - 1) * DEEP:levels * DEEP, :]
            ratio = near
            some_ratios, some_inverses, some_leads = [ratio], [None], [None]
            for b in range(1, lev):
                inverse = 1.0 / (1.0 - near * ratio)
                lead = distant * ratio * inverse
                ratio = near + lead * distant
                some_ratios.append(ratio)
                some_inverses.append(inverse)
                some_leads.append(lead)
            nears.append(near)
            distants.append(distant)
            ratios.append(some_ratios)
            inverses.append(some_inverses)
            leads.append(some_leads)
        for step in range(1, lev):
            end_copy(step, (block + lev - step) % lev, n).wait_recv()
        for i_k, k in enumerate(sections):
            near, distant = nears[i_k], distants[i_k]
            value = ends[0, k, DEEP:2 * DEEP, :]
            values = [value]
            for b in range(1, lev):
                first = ends[b, k, 0:DEEP, :] + near * value
                value = ends[b, k, DEEP:2 * DEEP, :] + distant * value + leads[i_k][b] * first
                values.append(value)
            follow = zeros
            first_val[lev, k] = follow
            last_val[0, k] = follow
            for b in range(lev - 1, 0, -1):
                follow = inverses[i_k][b] * (
                    ends[b, k, 0:DEEP, :] + near * values[b - 1] + distant * follow
                )
                first_val[b, k] = follow
                last_val[b, k] = values[b - 1] + ratios[i_k][b - 1] * follow
        below = [last_val[block, k] for k in sections]

        def up_pair(j, carry):
            rows = level_rows(levels - 2 - 2 * j, 2)
            after = []
            for i_k, k in enumerate(sections):
                both, inverse = own_part[k, rows, :], coef[k, rows, :]
                high = both[DEEP:] + inverse[DEEP:] * carry[i_k]
                low = both[:DEEP] + inverse[:DEEP] * high
                gain = from_lo[k, rows, :]
                own_part[k, rows, :] = jnp.concatenate(
                    [low + gain[:DEEP] * below[i_k], high + gain[DEEP:] * below[i_k]], axis=0
                )
                after.append(low)
            return tuple(after)

        over_pairs(
            up_pair, 0, levels // 2, tuple(first_val[block + 1, k] for k in sections)
        )
        tiles = KXM // 128
        for k in sections:
            for c in range(2):
                for j in range(PER):
                    out_ref[pl.ds(c * levels * tiles + k * PER + j, levels, stride=tiles), :] = (
                        own_part[k, pl.ds(c * PER + j, levels, stride=DEEP), :]
                    )

    for n in range(len(section_groups)):
        down_pass(n)
    for n in range(len(section_groups)):
        up_pass(n)

    to_prev.wait_send()
    to_next.wait_send()

    def lines_sent(d, carry):
        for which in range(2):
            for g in range(2):
                line_copy(d, which, g).wait_send()
        return carry

    lax.fori_loop(0, chain, lines_sent, 0)

    def flows_sent(s, carry):
        d, way = unit(s)
        for k in range(SECTIONS):
            for g in range(2):
                flow_copy(d, way, k, g).wait_send()
        return carry

    lax.fori_loop(0, chain - 1, flows_sent, 0)
    for n in range(len(section_groups)):
        for step in range(1, lev):
            end_copy(step, block, n).wait_send()


def solution(mesh):
    wide, lev = mesh.shape["wide"], mesh.shape["lev"]
    tables = make_tables()

    def local(nonlinear):
        _, _, levels, rows_ky, chunk = nonlinear.shape
        rows = levels * rows_ky
        halo_rows = max(16, rows_ky)
        chain = wide // 2
        f32, bf16 = jnp.float32, jnp.bfloat16
        dma = pltpu.SemaphoreType.DMA
        pressure = pl.pallas_call(
            functools.partial(kernel, wide, lev, rows_ky, levels),
            out_shape=pltpu.VMEM((2 * levels * KXM // 128, 128), f32),
            in_specs=[
                pl.BlockSpec(memory_space=pl.ANY),
                pl.BlockSpec(memory_space=pl.ANY),
            ],
            out_specs=pl.BlockSpec(memory_space=pltpu.VMEM),
            scratch_shapes=[
                pltpu.VMEM((3, 2, rows, chunk), bf16),
                pltpu.VMEM((2 * chunk, 2 * KXM), bf16),
                pltpu.VMEM((rows_ky, 4, levels, chunk), bf16),
                pltpu.VMEM((chain, 4, levels, chunk), bf16),
                pltpu.VMEM((2, halo_rows, chunk), bf16),
                pltpu.VMEM((2, halo_rows, chunk), bf16),
                pltpu.VMEM((2, rows + 2 * rows_ky, chunk), f32),
                pltpu.VMEM((SECTIONS, levels * DEEP, 128), f32),
                pltpu.VMEM((SECTIONS, levels * DEEP, 128), f32),
                pltpu.VMEM((chain, SECTIONS, (levels + 2) * DEEP, 128), bf16),
                pltpu.VMEM((chain + 1, SECTIONS, (levels + 2) * DEEP, 128), bf16),
                pltpu.VMEM((SECTIONS, levels * DEEP, 128), f32),
                pltpu.VMEM((SECTIONS, levels * DEEP, 128), f32),
                pltpu.VMEM((lev, SECTIONS, 2 * DEEP, 128), f32),
                pltpu.VMEM((lev + 1, SECTIONS, DEEP, 128), f32),
                pltpu.VMEM((lev + 1, SECTIONS, DEEP, 128), f32),
                pltpu.VMEM((SECTIONS, 2, DEEP, 128), f32),
                dma((3, 2)),
                dma((2, 4)),
                dma((2,)),
                dma((2,)),
                dma((2, 2, chain)),
                dma((2, 2, chain)),
                dma((chain, SECTIONS, 2)),
                dma((chain + 1, SECTIONS, 2)),
                dma((lev, 2)),
                dma((lev, 2)),
            ],
            compiler_params=pltpu.CompilerParams(
                collective_id=0, has_side_effects=True, vmem_limit_bytes=56 * 2**20
            ),
            cost_estimate=pl.CostEstimate(
                flops=2 * 4 * levels * NXG * 2 * KXM,
                bytes_accessed=2 * chunk * 2 * KXM * 2 + 4 * rows * chunk * 2,
                transcendentals=0,
            ),
        )(nonlinear.reshape(3, 2, rows, chunk), jnp.asarray(tables))
        return pressure.reshape(2, levels, 1, KXM)

    placed = (P(None, None, "lev", None, "wide"),)
    return jax.shard_map(
        local, mesh=mesh, in_specs=placed, out_specs=P(None, "lev", "wide", None), check_vma=False
    )
```

```python
import functools
import math

import jax
import jax.numpy as jnp
import ml_dtypes
import numpy as np
from jax import lax
from jax.experimental import pallas as pl
from jax.experimental.pallas import tpu as pltpu
from jax.sharding import PartitionSpec as P

NXG = 4096
KXM = 1536
MESH = pl.DeviceIdType.MESH
SEC = 512
TILE = 256
SECTIONS = KXM // SEC
PER = SEC // 128
DEEP = 2 * PER


def make_tables():
    places = np.arange(NXG, dtype=np.int32)
    waves = np.arange(KXM, dtype=np.int32) - KXM // 2
    phases = np.mod(places[:, None] * waves[None, :], NXG)
    turn = np.arange(NXG, dtype=np.float32) * np.float32(2.0 * math.pi / NXG)
    cosine = np.cos(turn).astype(ml_dtypes.bfloat16)[phases]
    sine = np.sin(turn).astype(ml_dtypes.bfloat16)[phases]
    return np.concatenate([cosine, sine], axis=1)


def level_rows(i, count=1):
    return pl.ds(pl.multiple_of(i * DEEP, DEEP), count * DEEP)


def kernel(
    wide, lev, rows_ky, levels,
    x_ref, tab_ref, out_ref,
    x_buf, tab, send, recv, halo_lo, halo_hi, zpad, part, own_part, flow_out, flow_in, coef, from_lo,
    ends, last_val, first_val, lost_val,
    x_sem, tab_sem, halo_send, halo_recv, send_sem, recv_sem, flow_send, flow_recv, end_send, end_recv,
):
    f32, bf16 = jnp.float32, jnp.bfloat16
    chunk = x_ref.shape[3]
    line_rows = levels * rows_ky
    half_levels = levels // 2
    group_levels = max(16, 256 // rows_ky)
    group_rows = group_levels * rows_ky
    groups = levels // group_levels
    halo_rows = halo_lo.shape[1]
    spacing = 2.0 * math.pi / NXG
    me = lax.axis_index("wide")
    block = lax.axis_index("lev")
    chain = wide // 2
    q, h = me // 2, me % 2
    pair = me + 1 - 2 * h
    has_prev = (q + chain - 1) // chain
    has_next = (2 * chain - 2 - q) // chain

    tab_parts = tab_sem.shape[1]
    tab_rows = chunk // tab_parts

    def tab_copy(side, i):
        at = pl.multiple_of((me if side == 0 else pair) * chunk + i * tab_rows, tab_rows)
        return pltpu.make_async_copy(
            tab_ref.at[pl.ds(at, tab_rows)],
            tab.at[pl.ds(side * chunk + i * tab_rows, tab_rows)],
            tab_sem.at[side, i],
        )

    barrier = pltpu.get_barrier_semaphore()
    pl.semaphore_signal(barrier, inc=1, device_id={"wide": pair}, device_id_type=MESH)

    @pl.when(q > 0)
    def _():
        pl.semaphore_signal(barrier, inc=1, device_id={"wide": me - 2}, device_id_type=MESH)

    @pl.when(q < chain - 1)
    def _():
        pl.semaphore_signal(barrier, inc=1, device_id={"wide": me + 2}, device_id_type=MESH)

    for step in range(1, lev):
        pl.semaphore_signal(
            barrier, inc=1, device_id={"lev": (block + step) % lev}, device_id_type=MESH
        )
    def x_copy(term, c):
        return pltpu.make_async_copy(x_ref.at[term, c], x_buf.at[term, c], x_sem.at[term, c])

    for term in (0, 2, 1):
        for c in range(2):
            x_copy(term, c).start()
    out_row = lax.broadcasted_iota(jnp.int32, (group_rows, group_rows), 0)
    in_row = lax.broadcasted_iota(jnp.int32, (group_rows, group_rows), 1)
    wanted = (out_row % group_levels) * rows_ky + out_row // group_levels
    shuffle = jnp.where(in_row == wanted, 1.0, 0.0).astype(bf16)

    def place(values, c, g):
        moved = jnp.dot(shuffle, values, preferred_element_type=f32).astype(bf16)
        for ky in range(rows_ky):
            send[ky, c, g * group_levels:(g + 1) * group_levels, :] = moved[
                ky * group_levels:(ky + 1) * group_levels
            ]

    upper_far = 1 - (2 * q) // chain
    far = upper_far * (chain - 1 - q) + (1 - upper_far) * q
    near_count = chain - 1 - far
    alone = far - near_count

    def unit(s):
        late = (s - alone + chain) // chain
        t = late * (s - alone)
        distance = (1 - late) * (far - s) + late * (near_count - t // 2)
        up = (1 - late) * upper_far + late * ((1 - upper_far) * (1 - t % 2) + upper_far * (t % 2))
        way = 2 * up - 1
        return q + way * distance, way

    def line_copy(d, which, g):
        rows = (pl.ds(2 * which, 2), pl.ds(g * half_levels, half_levels))
        return pltpu.make_async_remote_copy(
            src_ref=send.at[(2 * d + 1 - h,) + rows],
            dst_ref=recv.at[(d,) + rows],
            send_sem=send_sem.at[which, g, d],
            recv_sem=recv_sem.at[which, g, d],
            device_id={"wide": pair},
            device_id_type=MESH,
        )

    pl.semaphore_wait(barrier, lev + has_prev + has_next)
    to_prev = pltpu.make_async_remote_copy(
        src_ref=x_ref.at[2, :, 0:halo_rows],
        dst_ref=halo_hi,
        send_sem=halo_send.at[0],
        recv_sem=halo_recv.at[0],
        device_id={"lev": (block + lev - 1) % lev},
        device_id_type=MESH,
    )
    to_next = pltpu.make_async_remote_copy(
        src_ref=x_ref.at[2, :, line_rows - halo_rows:line_rows],
        dst_ref=halo_lo,
        send_sem=halo_send.at[1],
        recv_sem=halo_recv.at[1],
        device_id={"lev": (block + 1) % lev},
        device_id_type=MESH,
    )
    to_next.start()
    to_prev.start()

    first_unit, first_way = unit(0)
    for c in range(2):
        x_copy(0, c).wait()
    for part_of in range(2):
        for g in range(part_of * groups // 2, (part_of + 1) * groups // 2):
            for c in range(2):
                place(x_buf[0, c, g * group_rows:(g + 1) * group_rows, :], c, g)
        if part_of == 0:
            line_copy(first_unit, 0, 0).start()

    for c in range(2):
        x_copy(2, c).wait()
        zpad[c, rows_ky:rows_ky + line_rows, :] = x_buf[2, c].astype(f32)
    for c in range(2):
        x_copy(1, c).wait()
    for side in range(2):
        for i in range(tab_parts):
            tab_copy(side, i).start()
    ky_row = lax.broadcasted_iota(jnp.int32, (group_rows, chunk), 0) % rows_ky
    ky_scaled = ky_row.astype(f32) * spacing
    for part_of in range(2):
        if part_of == 0:
            to_next.wait_recv()
            for c in range(2):
                low = halo_lo[c].astype(f32)[halo_rows - rows_ky:]
                zpad[c, 0:rows_ky, :] = jnp.where(block > 0, low, 0.0)
        else:
            to_prev.wait_recv()
            for c in range(2):
                high = halo_hi[c].astype(f32)[:rows_ky]
                zpad[c, rows_ky + line_rows:, :] = jnp.where(block < lev - 1, high, 0.0)
        for g in range(part_of * groups // 2, (part_of + 1) * groups // 2):
            for c in range(2):
                at = g * group_rows
                upper = zpad[c, at + 2 * rows_ky:at + 2 * rows_ky + group_rows, :]
                lower = zpad[c, at:at + group_rows, :]
                turned = ky_scaled * x_buf[1, 1 - c, at:at + group_rows, :].astype(f32)
                slope = (upper - lower) * 0.5
                mixed = slope - turned if c == 0 else slope + turned
                place(mixed.astype(bf16), 2 + c, g)
        line_copy(first_unit, 1, part_of).start()
        if part_of == 0:
            line_copy(first_unit, 0, 1).start()

    def start_lines(d):
        for which in range(2):
            for g in range(2):
                line_copy(d, which, g).start()

    def send_lines(s, carry):
        d, _ = unit(s)
        start_lines(d)
        return carry

    lax.fori_loop(1, chain, send_lines, 0)

    def clear(slot):
        for k in range(SECTIONS):
            flow_in[slot, k] = jnp.zeros(flow_in.shape[2:], bf16)

    @pl.when(q == 0)
    def _():
        @pl.loop(0, chain)
        def _(slot):
            clear(slot)

    @pl.when(q == chain - 1)
    def _():
        @pl.loop(0, chain - 1)
        def _(slot):
            clear(slot)

        clear(chain)

    part_row = lax.broadcasted_iota(jnp.int32, (DEEP, 128), 0)
    lane = lax.broadcasted_iota(jnp.int32, (DEEP, 128), 1)

    def diagonal(ky, k):
        column = k * SEC + (part_row % PER) * 128 + lane
        kx = (column - KXM // 2).astype(f32) * spacing
        kyd = ky.astype(f32) * spacing
        return 2.0 + (kyd * kyd + kx * kx)

    own_diagonal = [diagonal(me, k) for k in range(SECTIONS)]

    def coef_step(i, carry):
        after = []
        for k in range(SECTIONS):
            shift, gain = carry[2 * k], carry[2 * k + 1]
            inverse = 1.0 / (own_diagonal[k] - shift)
            gain = gain * inverse
            coef[k, level_rows(i), :] = inverse
            from_lo[k, level_rows(i), :] = gain
            after += [inverse, gain]
        return tuple(after)

    zeros = jnp.zeros((DEEP, 128), f32)
    ones = jnp.ones((DEEP, 128), f32)
    lax.fori_loop(0, levels, coef_step, (zeros, ones) * SECTIONS)

    def unit_step(j, carry):
        i = levels - 1 - j
        after = []
        for k in range(SECTIONS):
            low = from_lo[k, level_rows(i), :] + coef[k, level_rows(i), :] * carry[k]
            from_lo[k, level_rows(i), :] = low
            after.append(low)
        return tuple(after)

    lax.fori_loop(0, levels, unit_step, (zeros,) * SECTIONS)

    for side in range(2):
        for i in range(tab_parts):
            tab_copy(side, i).wait()

    norm_scale = 1.0 / math.sqrt(NXG)

    def transform(target, k, begin, n, holders, table):
        rows = slice(begin, begin + n)
        lines = jnp.concatenate(
            [holder[:, rows, :].reshape(4 * n, chunk) for holder in holders], axis=1
        )
        for t in range(SEC // TILE):
            first = k * SEC + t * TILE
            cos_at, sin_at = pl.multiple_of(first, TILE), pl.multiple_of(KXM + first, TILE)
            with_cos = jnp.dot(
                lines, table[:, pl.ds(cos_at, TILE)], preferred_element_type=f32
            )
            with_sin = jnp.dot(
                lines, table[:, pl.ds(sin_at, TILE)], preferred_element_type=f32
            )
            kx = (
                lax.broadcasted_iota(jnp.int32, (1, TILE), 1) + first - KXM // 2
            ).astype(f32) * spacing
            fx_real = (with_cos[0:n] + with_sin[n:2 * n]) * norm_scale
            fx_imag = (with_cos[n:2 * n] - with_sin[0:n]) * norm_scale
            fg_real = (with_cos[2 * n:3 * n] + with_sin[3 * n:4 * n]) * norm_scale
            fg_imag = (with_cos[3 * n:4 * n] - with_sin[2 * n:3 * n]) * norm_scale
            source_real = kx * fx_imag - fg_real
            source_imag = -kx * fx_real - fg_imag
            for j in range(TILE // 128):
                at = slice(j * 128, (j + 1) * 128)
                place_at = begin * DEEP + t * (TILE // 128) + j
                for c, source in ((0, source_real), (1, source_imag)):
                    where = pl.ds(c * PER + place_at, n, stride=DEEP)
                    target[k, where, :] = source[:, at]

    def transform_unit(d, k, begin, n):
        transform(part, k, begin, n, [send.at[2 * d + h], recv.at[d]], tab)

    def has_rest(k):
        return k * SEC < KXM // 2 < (k + 1) * SEC

    def flow_rows(k, g):
        return pl.ds(g * half_levels * DEEP, (half_levels + 2 * (g * has_rest(k))) * DEEP)


    def flow_copy(d, way, k, g):
        slot = jnp.where(q + way == d, jnp.where(way > 0, d, chain), d)
        return pltpu.make_async_remote_copy(
            src_ref=flow_out.at[d, k, flow_rows(k, g)],
            dst_ref=flow_in.at[slot, k, flow_rows(k, g)],
            send_sem=flow_send.at[d, k, g],
            recv_sem=flow_recv.at[slot, k, g],
            device_id={"wide": me + 2 * way},
            device_id_type=MESH,
        )

    def arrival(slot, k, g):
        return pltpu.make_async_remote_copy(
            src_ref=flow_out.at[0, k, flow_rows(k, g)],
            dst_ref=flow_in.at[slot, k, flow_rows(k, g)],
            send_sem=flow_send.at[0, k, g],
            recv_sem=flow_recv.at[slot, k, g],
            device_id={"wide": pair},
            device_id_type=MESH,
        )

    def over_pairs(body, begin, count, carry):
        group = max(n for n in range(1, 9) if count % n == 0)

        def some(j, carry):
            for i in range(group):
                carry = body(begin + j * group + i, carry)
            return carry

        return lax.fori_loop(0, count // group, some, carry)

    half_pairs = half_levels // 2

    def rounded(value):
        return value.astype(bf16).astype(f32)

    def shape_noise(d, k, g, carry):
        diag = diagonal(2 * d + h, k)
        root = 0.5 * (diag - jnp.sqrt(jnp.maximum(diag * diag - 4.0, 0.0)))
        once, twice = 2.0 * root, root * root

        def one_pair(i, carry):
            lost, older = carry
            rows = level_rows(2 * i, 2)
            both = part[k, rows, :] + flow_in[d, k, rows, :].astype(f32)
            value = both[:DEEP] + (once * lost - twice * older)
            low = rounded(value)
            lost, older = value - low, lost
            value = both[DEEP:] + (once * lost - twice * older)
            high = rounded(value)
            lost, older = value - high, lost
            flow_out[d, k, rows, :] = jnp.concatenate([low, high], axis=0).astype(bf16)
            return lost, older

        if g == 0:
            return over_pairs(one_pair, 0, half_pairs, carry)
        if not has_rest(k):
            return over_pairs(one_pair, half_pairs, half_pairs, carry)
        lost, older = over_pairs(one_pair, half_pairs, half_pairs - 1, carry)
        rows, rest = pl.ds((levels - 2) * DEEP, 2 * DEEP), pl.ds(levels * DEEP, 2 * DEEP)
        both = part[k, rows, :] + flow_in[d, k, rows, :].astype(f32)
        both = both + flow_in[d, k, rest, :].astype(f32)
        both = both + jnp.concatenate([once * lost - twice * older, -(twice * lost)], axis=0)
        kept = rounded(both)
        flow_out[d, k, rows, :] = kept.astype(bf16)
        flow_out[d, k, rest, :] = (both - kept).astype(bf16)
        return carry

    def await_flow(d, way, k, g):
        before = q - way

        @pl.when(jnp.logical_and(before >= 0, before < chain))
        def _():
            arrival(d, k, g).wait_recv()

    def await_lines(d, g):
        for which in range(2):
            line_copy(d, which, g).wait_recv()

    for g in range(2):
        await_lines(first_unit, g)
        for k in range(SECTIONS):
            transform_unit(first_unit, k, g * half_levels, half_levels)
            await_flow(first_unit, first_way, k, g)
            if g == 0:
                lost, older = shape_noise(first_unit, k, g, (zeros, zeros))
                lost_val[k, 0] = lost
                lost_val[k, 1] = older
            else:
                shape_noise(first_unit, k, g, (lost_val[k, 0], lost_val[k, 1]))
            flow_copy(first_unit, first_way, k, g).start()

    def pass_unit(d, way):
        for k in range(SECTIONS):
            transform_unit(d, k, 0, levels)
            lost = (zeros, zeros)
            for g in range(2):
                await_flow(d, way, k, g)
                lost = shape_noise(d, k, g, lost)
                flow_copy(d, way, k, g).start()

    def pass_on(s, carry):
        d, way = unit(s)
        await_lines(d, 0)
        await_lines(d, 1)
        pass_unit(d, way)
        return carry

    lax.fori_loop(1, chain - 1, pass_on, 0)
    await_lines(q, 0)
    await_lines(q, 1)

    @pl.loop(0, SECTIONS)
    def _(k):
        transform(own_part, k, 0, levels, [send.at[me], recv.at[q]], tab)

    section_groups = (range(SECTIONS - 1), range(SECTIONS - 1, SECTIONS))

    def end_copy(step, slot, n):
        sections = pl.ds(section_groups[n][0], len(section_groups[n]))
        return pltpu.make_async_remote_copy(
            src_ref=ends.at[slot, sections],
            dst_ref=ends.at[slot, sections],
            send_sem=end_send.at[step, n],
            recv_sem=end_recv.at[step, n],
            device_id={"lev": (block + step) % lev},
            device_id_type=MESH,
        )

    def down_pass(n):
        sections = section_groups[n]

        def down_pair(i, carry):
            rows = level_rows(2 * i, 2)
            after = []
            for i_k, k in enumerate(sections):
                value, first = carry[2 * i_k], carry[2 * i_k + 1]
                both = own_part[k, rows, :] + (
                    flow_in[q, k, rows, :].astype(f32) + flow_in[chain, k, rows, :].astype(f32)
                )
                weighted = from_lo[k, rows, :] * both
                first = first + (weighted[:DEEP] + weighted[DEEP:])
                inverse = coef[k, rows, :]
                low = (both[:DEEP] + value) * inverse[:DEEP]
                high = (both[DEEP:] + low) * inverse[DEEP:]
                own_part[k, rows, :] = jnp.concatenate([low, high], axis=0)
                after += [high, first]
            return tuple(after)

        carry = (zeros, zeros) * len(sections)
        for g in range(2):
            for k in sections:
                @pl.when(q > 0)
                def _():
                    arrival(q, k, g).wait_recv()

                @pl.when(q < chain - 1)
                def _():
                    arrival(chain, k, g).wait_recv()

                if g == 1 and has_rest(k):
                    rows = pl.ds((levels - 2) * DEEP, 2 * DEEP)
                    rest = pl.ds(levels * DEEP, 2 * DEEP)
                    own_part[k, rows, :] = own_part[k, rows, :] + (
                        flow_in[q, k, rest, :].astype(f32)
                        + flow_in[chain, k, rest, :].astype(f32)
                    )
            carry = over_pairs(down_pair, g * half_pairs, half_pairs, carry)
        for i_k, k in enumerate(sections):
            ends[block, k, 0:DEEP, :] = carry[2 * i_k + 1]
            ends[block, k, DEEP:2 * DEEP, :] = carry[2 * i_k]
        for step in range(1, lev):
            end_copy(step, block, n).start()

    def up_pass(n):
        sections = section_groups[n]
        nears, distants, ratios, inverses, leads = [], [], [], [], []
        for k in sections:
            near = from_lo[k, 0:DEEP, :]
            distant = from_lo[k, (levels - 1) * DEEP:levels * DEEP, :]
            ratio = near
            some_ratios, some_inverses, some_leads = [ratio], [None], [None]
            for b in range(1, lev):
                inverse = 1.0 / (1.0 - near * ratio)
                lead = distant * ratio * inverse
                ratio = near + lead * distant
                some_ratios.append(ratio)
                some_inverses.append(inverse)
                some_leads.append(lead)
            nears.append(near)
            distants.append(distant)
            ratios.append(some_ratios)
            inverses.append(some_inverses)
            leads.append(some_leads)
        for step in range(1, lev):
            end_copy(step, (block + lev - step) % lev, n).wait_recv()
        for i_k, k in enumerate(sections):
            near, distant = nears[i_k], distants[i_k]
            value = ends[0, k, DEEP:2 * DEEP, :]
            values = [value]
            for b in range(1, lev):
                first = ends[b, k, 0:DEEP, :] + near * value
                value = ends[b, k, DEEP:2 * DEEP, :] + distant * value + leads[i_k][b] * first
                values.append(value)
            follow = zeros
            first_val[lev, k] = follow
            last_val[0, k] = follow
            for b in range(lev - 1, 0, -1):
                follow = inverses[i_k][b] * (
                    ends[b, k, 0:DEEP, :] + near * values[b - 1] + distant * follow
                )
                first_val[b, k] = follow
                last_val[b, k] = values[b - 1] + ratios[i_k][b - 1] * follow
        below = [last_val[block, k] for k in sections]

        def up_pair(j, carry):
            rows = level_rows(levels - 2 - 2 * j, 2)
            after = []
            for i_k, k in enumerate(sections):
                both, inverse = own_part[k, rows, :], coef[k, rows, :]
                high = both[DEEP:] + inverse[DEEP:] * carry[i_k]
                low = both[:DEEP] + inverse[:DEEP] * high
                gain = from_lo[k, rows, :]
                own_part[k, rows, :] = jnp.concatenate(
                    [low + gain[:DEEP] * below[i_k], high + gain[DEEP:] * below[i_k]], axis=0
                )
                after.append(low)
            return tuple(after)

        over_pairs(
            up_pair, 0, levels // 2, tuple(first_val[block + 1, k] for k in sections)
        )
        tiles = KXM // 128
        for k in sections:
            for c in range(2):
                for j in range(PER):
                    out_ref[pl.ds(c * levels * tiles + k * PER + j, levels, stride=tiles), :] = (
                        own_part[k, pl.ds(c * PER + j, levels, stride=DEEP), :]
                    )

    for n in range(len(section_groups)):
        down_pass(n)
    for n in range(len(section_groups)):
        up_pass(n)

    to_prev.wait_send()
    to_next.wait_send()

    def lines_sent(d, carry):
        for which in range(2):
            for g in range(2):
                line_copy(d, which, g).wait_send()
        return carry

    lax.fori_loop(0, chain, lines_sent, 0)

    def flows_sent(s, carry):
        d, way = unit(s)
        for k in range(SECTIONS):
            for g in range(2):
                flow_copy(d, way, k, g).wait_send()
        return carry

    lax.fori_loop(0, chain - 1, flows_sent, 0)
    for n in range(len(section_groups)):
        for step in range(1, lev):
            end_copy(step, block, n).wait_send()


def solution(mesh):
    wide, lev = mesh.shape["wide"], mesh.shape["lev"]
    tables = make_tables()

    def local(nonlinear):
        _, _, levels, rows_ky, chunk = nonlinear.shape
        rows = levels * rows_ky
        halo_rows = max(16, rows_ky)
        chain = wide // 2
        f32, bf16 = jnp.float32, jnp.bfloat16
        dma = pltpu.SemaphoreType.DMA
        pressure = pl.pallas_call(
            functools.partial(kernel, wide, lev, rows_ky, levels),
            out_shape=pltpu.VMEM((2 * levels * KXM // 128, 128), f32),
            in_specs=[
                pl.BlockSpec(memory_space=pl.ANY),
                pl.BlockSpec(memory_space=pl.ANY),
            ],
            out_specs=pl.BlockSpec(memory_space=pltpu.VMEM),
            scratch_shapes=[
                pltpu.VMEM((3, 2, rows, chunk), bf16),
                pltpu.VMEM((2 * chunk, 2 * KXM), bf16),
                pltpu.VMEM((rows_ky, 4, levels, chunk), bf16),
                pltpu.VMEM((chain, 4, levels, chunk), bf16),
                pltpu.VMEM((2, halo_rows, chunk), bf16),
                pltpu.VMEM((2, halo_rows, chunk), bf16),
                pltpu.VMEM((2, rows + 2 * rows_ky, chunk), f32),
                pltpu.VMEM((SECTIONS, levels * DEEP, 128), f32),
                pltpu.VMEM((SECTIONS, levels * DEEP, 128), f32),
                pltpu.VMEM((chain, SECTIONS, (levels + 2) * DEEP, 128), bf16),
                pltpu.VMEM((chain + 1, SECTIONS, (levels + 2) * DEEP, 128), bf16),
                pltpu.VMEM((SECTIONS, levels * DEEP, 128), f32),
                pltpu.VMEM((SECTIONS, levels * DEEP, 128), f32),
                pltpu.VMEM((lev, SECTIONS, 2 * DEEP, 128), f32),
                pltpu.VMEM((lev + 1, SECTIONS, DEEP, 128), f32),
                pltpu.VMEM((lev + 1, SECTIONS, DEEP, 128), f32),
                pltpu.VMEM((SECTIONS, 2, DEEP, 128), f32),
                dma((3, 2)),
                dma((2, 4)),
                dma((2,)),
                dma((2,)),
                dma((2, 2, chain)),
                dma((2, 2, chain)),
                dma((chain, SECTIONS, 2)),
                dma((chain + 1, SECTIONS, 2)),
                dma((lev, 2)),
                dma((lev, 2)),
            ],
            compiler_params=pltpu.CompilerParams(
                collective_id=0, has_side_effects=True, vmem_limit_bytes=56 * 2**20
            ),
            cost_estimate=pl.CostEstimate(
                flops=2 * 4 * levels * NXG * 2 * KXM,
                bytes_accessed=2 * chunk * 2 * KXM * 2 + 4 * rows * chunk * 2,
                transcendentals=0,
            ),
        )(nonlinear.reshape(3, 2, rows, chunk), jnp.asarray(tables))
        return pressure.reshape(2, levels, 1, KXM)

    placed = (P(None, None, "lev", None, "wide"),)
    return jax.shard_map(
        local, mesh=mesh, in_specs=placed, out_specs=P(None, "lev", "wide", None), check_vma=False
    )
```

```python
import functools
import math

import jax
import jax.numpy as jnp
import ml_dtypes
import numpy as np
from jax import lax
from jax.experimental import pallas as pl
from jax.experimental.pallas import tpu as pltpu
from jax.sharding import PartitionSpec as P

NXG = 4096
KXM = 1536
MESH = pl.DeviceIdType.MESH
SEC = 512
TILE = 512
SECTIONS = KXM // SEC
PER = SEC // 128
DEEP = 2 * PER


def make_tables():
    places = np.arange(NXG, dtype=np.int32)
    waves = np.arange(KXM, dtype=np.int32) - KXM // 2
    phases = np.mod(places[:, None] * waves[None, :], NXG)
    turn = np.arange(NXG, dtype=np.float32) * np.float32(2.0 * math.pi / NXG)
    cosine = np.cos(turn).astype(ml_dtypes.bfloat16)[phases]
    sine = np.sin(turn).astype(ml_dtypes.bfloat16)[phases]
    return np.concatenate([cosine, sine], axis=1)


def level_rows(i, count=1):
    return pl.ds(pl.multiple_of(i * DEEP, DEEP), count * DEEP)


def kernel(
    wide, lev, rows_ky, levels,
    x_ref, tab_ref, out_ref,
    x_buf, tab, send, recv, halo_lo, halo_hi, zpad, part, own_part, flow_out, flow_in, coef, from_lo,
    ends, last_val, first_val, lost_val,
    x_sem, tab_sem, halo_send, halo_recv, send_sem, recv_sem, flow_send, flow_recv, end_send, end_recv,
):
    f32, bf16 = jnp.float32, jnp.bfloat16
    chunk = x_ref.shape[3]
    line_rows = levels * rows_ky
    half_levels = levels // 2
    group_levels = max(16, 256 // rows_ky)
    group_rows = group_levels * rows_ky
    groups = levels // group_levels
    halo_rows = halo_lo.shape[1]
    spacing = 2.0 * math.pi / NXG
    me = lax.axis_index("wide")
    block = lax.axis_index("lev")
    chain = wide // 2
    q, h = me // 2, me % 2
    pair = me + 1 - 2 * h
    has_prev = (q + chain - 1) // chain
    has_next = (2 * chain - 2 - q) // chain

    tab_parts = tab_sem.shape[1]
    tab_rows = chunk // tab_parts

    def tab_copy(side, i):
        at = pl.multiple_of((me if side == 0 else pair) * chunk + i * tab_rows, tab_rows)
        return pltpu.make_async_copy(
            tab_ref.at[pl.ds(at, tab_rows)],
            tab.at[pl.ds(side * chunk + i * tab_rows, tab_rows)],
            tab_sem.at[side, i],
        )

    barrier = pltpu.get_barrier_semaphore()
    pl.semaphore_signal(barrier, inc=1, device_id={"wide": pair}, device_id_type=MESH)

    @pl.when(q > 0)
    def _():
        pl.semaphore_signal(barrier, inc=1, device_id={"wide": me - 2}, device_id_type=MESH)

    @pl.when(q < chain - 1)
    def _():
        pl.semaphore_signal(barrier, inc=1, device_id={"wide": me + 2}, device_id_type=MESH)

    for step in range(1, lev):
        pl.semaphore_signal(
            barrier, inc=1, device_id={"lev": (block + step) % lev}, device_id_type=MESH
        )
    def x_copy(term, c):
        return pltpu.make_async_copy(x_ref.at[term, c], x_buf.at[term, c], x_sem.at[term, c])

    for term in (0, 2, 1):
        for c in range(2):
            x_copy(term, c).start()
    out_row = lax.broadcasted_iota(jnp.int32, (group_rows, group_rows), 0)
    in_row = lax.broadcasted_iota(jnp.int32, (group_rows, group_rows), 1)
    wanted = (out_row % group_levels) * rows_ky + out_row // group_levels
    shuffle = jnp.where(in_row == wanted, 1.0, 0.0).astype(bf16)

    def place(values, c, g):
        moved = jnp.dot(shuffle, values, preferred_element_type=f32).astype(bf16)
        for ky in range(rows_ky):
            send[ky, c, g * group_levels:(g + 1) * group_levels, :] = moved[
                ky * group_levels:(ky + 1) * group_levels
            ]

    upper_far = 1 - (2 * q) // chain
    far = upper_far * (chain - 1 - q) + (1 - upper_far) * q
    near_count = chain - 1 - far
    alone = far - near_count

    def unit(s):
        late = (s - alone + chain) // chain
        t = late * (s - alone)
        distance = (1 - late) * (far - s) + late * (near_count - t // 2)
        up = (1 - late) * upper_far + late * ((1 - upper_far) * (1 - t % 2) + upper_far * (t % 2))
        way = 2 * up - 1
        return q + way * distance, way

    def line_copy(d, which, g):
        rows = (pl.ds(2 * which, 2), pl.ds(g * half_levels, half_levels))
        return pltpu.make_async_remote_copy(
            src_ref=send.at[(2 * d + 1 - h,) + rows],
            dst_ref=recv.at[(d,) + rows],
            send_sem=send_sem.at[which, g, d],
            recv_sem=recv_sem.at[which, g, d],
            device_id={"wide": pair},
            device_id_type=MESH,
        )

    pl.semaphore_wait(barrier, lev + has_prev + has_next)
    to_prev = pltpu.make_async_remote_copy(
        src_ref=x_ref.at[2, :, 0:halo_rows],
        dst_ref=halo_hi,
        send_sem=halo_send.at[0],
        recv_sem=halo_recv.at[0],
        device_id={"lev": (block + lev - 1) % lev},
        device_id_type=MESH,
    )
    to_next = pltpu.make_async_remote_copy(
        src_ref=x_ref.at[2, :, line_rows - halo_rows:line_rows],
        dst_ref=halo_lo,
        send_sem=halo_send.at[1],
        recv_sem=halo_recv.at[1],
        device_id={"lev": (block + 1) % lev},
        device_id_type=MESH,
    )
    to_next.start()
    to_prev.start()

    first_unit, first_way = unit(0)
    for c in range(2):
        x_copy(0, c).wait()

    def place_x(part_of):
        for g in range(part_of * groups // 2, (part_of + 1) * groups // 2):
            for c in range(2):
                place(x_buf[0, c, g * group_rows:(g + 1) * group_rows, :], c, g)
        line_copy(first_unit, 0, part_of).start()

    place_x(0)

    for c in range(2):
        x_copy(2, c).wait()
    for c in range(2):
        x_copy(1, c).wait()
    for side in range(2):
        for i in range(tab_parts):
            tab_copy(side, i).start()
    ky_row = lax.broadcasted_iota(jnp.int32, (group_rows, chunk), 0) % rows_ky
    ky_scaled = ky_row.astype(f32) * spacing
    early_rows = (half_levels + 2) * rows_ky
    for part_of in range(2):
        begin, end = ((0, early_rows), (early_rows, line_rows))[part_of]
        for c in range(2):
            zpad[c, rows_ky + begin:rows_ky + end, :] = x_buf[2, c, begin:end, :].astype(f32)
        if part_of == 0:
            to_next.wait_recv()
            for c in range(2):
                low = halo_lo[c].astype(f32)[halo_rows - rows_ky:]
                zpad[c, 0:rows_ky, :] = jnp.where(block > 0, low, 0.0)
        else:
            to_prev.wait_recv()
            for c in range(2):
                high = halo_hi[c].astype(f32)[:rows_ky]
                zpad[c, rows_ky + line_rows:, :] = jnp.where(block < lev - 1, high, 0.0)
        for g in range(part_of * groups // 2, (part_of + 1) * groups // 2):
            for c in range(2):
                at = g * group_rows
                upper = zpad[c, at + 2 * rows_ky:at + 2 * rows_ky + group_rows, :]
                lower = zpad[c, at:at + group_rows, :]
                turned = ky_scaled * x_buf[1, 1 - c, at:at + group_rows, :].astype(f32)
                slope = (upper - lower) * 0.5
                mixed = slope - turned if c == 0 else slope + turned
                place(mixed.astype(bf16), 2 + c, g)
        line_copy(first_unit, 1, part_of).start()
        if part_of == 0:
            place_x(1)

    def start_lines(d):
        for which in range(2):
            for g in range(2):
                line_copy(d, which, g).start()

    def send_lines(s, carry):
        d, _ = unit(s)
        start_lines(d)
        return carry

    lax.fori_loop(1, chain, send_lines, 0)

    def clear(slot):
        for k in range(SECTIONS):
            flow_in[slot, k] = jnp.zeros(flow_in.shape[2:], bf16)

    @pl.when(q == 0)
    def _():
        @pl.loop(0, chain)
        def _(slot):
            clear(slot)

    @pl.when(q == chain - 1)
    def _():
        @pl.loop(0, chain - 1)
        def _(slot):
            clear(slot)

        clear(chain)

    part_row = lax.broadcasted_iota(jnp.int32, (DEEP, 128), 0)
    lane = lax.broadcasted_iota(jnp.int32, (DEEP, 128), 1)

    def diagonal(ky, k):
        column = k * SEC + (part_row % PER) * 128 + lane
        kx = (column - KXM // 2).astype(f32) * spacing
        kyd = ky.astype(f32) * spacing
        return 2.0 + (kyd * kyd + kx * kx)

    own_diagonal = [diagonal(me, k) for k in range(SECTIONS)]

    def coef_step(i, carry):
        after = []
        for k in range(SECTIONS):
            shift, gain = carry[2 * k], carry[2 * k + 1]
            inverse = 1.0 / (own_diagonal[k] - shift)
            gain = gain * inverse
            coef[k, level_rows(i), :] = inverse
            from_lo[k, level_rows(i), :] = gain
            after += [inverse, gain]
        return tuple(after)

    zeros = jnp.zeros((DEEP, 128), f32)
    ones = jnp.ones((DEEP, 128), f32)
    lax.fori_loop(0, levels, coef_step, (zeros, ones) * SECTIONS)

    def unit_step(j, carry):
        i = levels - 1 - j
        after = []
        for k in range(SECTIONS):
            low = from_lo[k, level_rows(i), :] + coef[k, level_rows(i), :] * carry[k]
            from_lo[k, level_rows(i), :] = low
            after.append(low)
        return tuple(after)

    lax.fori_loop(0, levels, unit_step, (zeros,) * SECTIONS)

    for side in range(2):
        for i in range(tab_parts):
            tab_copy(side, i).wait()

    norm_scale = 1.0 / math.sqrt(NXG)

    def transform(target, k, begin, n, holders, table):
        rows = slice(begin, begin + n)
        lines = jnp.concatenate(
            [holder[:, rows, :].reshape(4 * n, chunk) for holder in holders], axis=1
        )
        for t in range(SEC // TILE):
            first = k * SEC + t * TILE
            cos_at, sin_at = pl.multiple_of(first, TILE), pl.multiple_of(KXM + first, TILE)
            with_cos = jnp.dot(
                lines, table[:, pl.ds(cos_at, TILE)], preferred_element_type=f32
            )
            with_sin = jnp.dot(
                lines, table[:, pl.ds(sin_at, TILE)], preferred_element_type=f32
            )
            kx = (
                lax.broadcasted_iota(jnp.int32, (1, TILE), 1) + first - KXM // 2
            ).astype(f32) * spacing
            fx_real = (with_cos[0:n] + with_sin[n:2 * n]) * norm_scale
            fx_imag = (with_cos[n:2 * n] - with_sin[0:n]) * norm_scale
            fg_real = (with_cos[2 * n:3 * n] + with_sin[3 * n:4 * n]) * norm_scale
            fg_imag = (with_cos[3 * n:4 * n] - with_sin[2 * n:3 * n]) * norm_scale
            source_real = kx * fx_imag - fg_real
            source_imag = -kx * fx_real - fg_imag
            for j in range(TILE // 128):
                at = slice(j * 128, (j + 1) * 128)
                place_at = begin * DEEP + t * (TILE // 128) + j
                for c, source in ((0, source_real), (1, source_imag)):
                    where = pl.ds(c * PER + place_at, n, stride=DEEP)
                    target[k, where, :] = source[:, at]

    def transform_unit(d, k, begin, n):
        transform(part, k, begin, n, [send.at[2 * d + h], recv.at[d]], tab)

    def has_rest(k):
        return k * SEC < KXM // 2 < (k + 1) * SEC

    def flow_rows(k, g):
        return pl.ds(g * half_levels * DEEP, (half_levels + 2 * (g * has_rest(k))) * DEEP)


    def flow_copy(d, way, k, g):
        slot = jnp.where(q + way == d, jnp.where(way > 0, d, chain), d)
        return pltpu.make_async_remote_copy(
            src_ref=flow_out.at[d, k, flow_rows(k, g)],
            dst_ref=flow_in.at[slot, k, flow_rows(k, g)],
            send_sem=flow_send.at[d, k, g],
            recv_sem=flow_recv.at[slot, k, g],
            device_id={"wide": me + 2 * way},
            device_id_type=MESH,
        )

    def arrival(slot, k, g):
        return pltpu.make_async_remote_copy(
            src_ref=flow_out.at[0, k, flow_rows(k, g)],
            dst_ref=flow_in.at[slot, k, flow_rows(k, g)],
            send_sem=flow_send.at[0, k, g],
            recv_sem=flow_recv.at[slot, k, g],
            device_id={"wide": pair},
            device_id_type=MESH,
        )

    def over_pairs(body, begin, count, carry):
        group = max(n for n in range(1, 17) if count % n == 0)

        def some(j, carry):
            for i in range(group):
                carry = body(begin + j * group + i, carry)
            return carry

        return lax.fori_loop(0, count // group, some, carry)

    half_pairs = half_levels // 2

    def rounded(value):
        return value.astype(bf16).astype(f32)

    def shape_noise(d, k, g, carry):
        diag = diagonal(2 * d + h, k)
        root = 0.5 * (diag - jnp.sqrt(jnp.maximum(diag * diag - 4.0, 0.0)))
        once, twice = 2.0 * root, root * root

        def one_pair(i, carry):
            lost, older = carry
            rows = level_rows(2 * i, 2)
            both = part[k, rows, :] + flow_in[d, k, rows, :].astype(f32)
            value = both[:DEEP] + (once * lost - twice * older)
            low = rounded(value)
            lost, older = value - low, lost
            value = both[DEEP:] + (once * lost - twice * older)
            high = rounded(value)
            lost, older = value - high, lost
            flow_out[d, k, rows, :] = jnp.concatenate([low, high], axis=0).astype(bf16)
            return lost, older

        if g == 0:
            return over_pairs(one_pair, 0, half_pairs, carry)
        if not has_rest(k):
            return over_pairs(one_pair, half_pairs, half_pairs, carry)
        lost, older = over_pairs(one_pair, half_pairs, half_pairs - 1, carry)
        rows, rest = pl.ds((levels - 2) * DEEP, 2 * DEEP), pl.ds(levels * DEEP, 2 * DEEP)
        both = part[k, rows, :] + flow_in[d, k, rows, :].astype(f32)
        both = both + flow_in[d, k, rest, :].astype(f32)
        both = both + jnp.concatenate([once * lost - twice * older, -(twice * lost)], axis=0)
        kept = rounded(both)
        flow_out[d, k, rows, :] = kept.astype(bf16)
        flow_out[d, k, rest, :] = (both - kept).astype(bf16)
        return carry

    def await_flow(d, way, k, g):
        before = q - way

        @pl.when(jnp.logical_and(before >= 0, before < chain))
        def _():
            arrival(d, k, g).wait_recv()

    def await_lines(d, g):
        for which in range(2):
            line_copy(d, which, g).wait_recv()

    for g in range(2):
        await_lines(first_unit, g)
        for k in range(SECTIONS):
            transform_unit(first_unit, k, g * half_levels, half_levels)
            await_flow(first_unit, first_way, k, g)
            if g == 0:
                lost, older = shape_noise(first_unit, k, g, (zeros, zeros))
                lost_val[k, 0] = lost
                lost_val[k, 1] = older
            else:
                shape_noise(first_unit, k, g, (lost_val[k, 0], lost_val[k, 1]))
            flow_copy(first_unit, first_way, k, g).start()

    def pass_unit(d, way):
        for k in range(SECTIONS):
            transform_unit(d, k, 0, levels)
            lost = (zeros, zeros)
            for g in range(2):
                await_flow(d, way, k, g)
                lost = shape_noise(d, k, g, lost)
                flow_copy(d, way, k, g).start()

    def pass_on(s, carry):
        d, way = unit(s)
        await_lines(d, 0)
        await_lines(d, 1)
        pass_unit(d, way)
        return carry

    lax.fori_loop(1, chain - 1, pass_on, 0)
    await_lines(q, 0)
    await_lines(q, 1)

    @pl.loop(0, SECTIONS)
    def _(k):
        transform(own_part, k, 0, levels, [send.at[me], recv.at[q]], tab)

    section_groups = (range(SECTIONS - 1), range(SECTIONS - 1, SECTIONS))

    def end_copy(step, slot, n):
        sections = pl.ds(section_groups[n][0], len(section_groups[n]))
        return pltpu.make_async_remote_copy(
            src_ref=ends.at[slot, sections],
            dst_ref=ends.at[slot, sections],
            send_sem=end_send.at[step, n],
            recv_sem=end_recv.at[step, n],
            device_id={"lev": (block + step) % lev},
            device_id_type=MESH,
        )

    def down_pass(n):
        sections = section_groups[n]

        def down_pair(i, carry):
            rows = level_rows(2 * i, 2)
            after = []
            for i_k, k in enumerate(sections):
                value, first = carry[2 * i_k], carry[2 * i_k + 1]
                both = own_part[k, rows, :] + (
                    flow_in[q, k, rows, :].astype(f32) + flow_in[chain, k, rows, :].astype(f32)
                )
                weighted = from_lo[k, rows, :] * both
                first = first + (weighted[:DEEP] + weighted[DEEP:])
                inverse = coef[k, rows, :]
                low = (both[:DEEP] + value) * inverse[:DEEP]
                high = (both[DEEP:] + low) * inverse[DEEP:]
                own_part[k, rows, :] = jnp.concatenate([low, high], axis=0)
                after += [high, first]
            return tuple(after)

        carry = (zeros, zeros) * len(sections)
        for g in range(2):
            for k in sections:
                @pl.when(q > 0)
                def _():
                    arrival(q, k, g).wait_recv()

                @pl.when(q < chain - 1)
                def _():
                    arrival(chain, k, g).wait_recv()

                if g == 1 and has_rest(k):
                    rows = pl.ds((levels - 2) * DEEP, 2 * DEEP)
                    rest = pl.ds(levels * DEEP, 2 * DEEP)
                    own_part[k, rows, :] = own_part[k, rows, :] + (
                        flow_in[q, k, rest, :].astype(f32)
                        + flow_in[chain, k, rest, :].astype(f32)
                    )
            carry = over_pairs(down_pair, g * half_pairs, half_pairs, carry)
        for i_k, k in enumerate(sections):
            ends[block, k, 0:DEEP, :] = carry[2 * i_k + 1]
            ends[block, k, DEEP:2 * DEEP, :] = carry[2 * i_k]
        for step in range(1, lev):
            end_copy(step, block, n).start()

    def up_pass(n):
        sections = section_groups[n]
        nears, distants, ratios, inverses, leads = [], [], [], [], []
        for k in sections:
            near = from_lo[k, 0:DEEP, :]
            distant = from_lo[k, (levels - 1) * DEEP:levels * DEEP, :]
            ratio = near
            some_ratios, some_inverses, some_leads = [ratio], [None], [None]
            for b in range(1, lev):
                inverse = 1.0 / (1.0 - near * ratio)
                lead = distant * ratio * inverse
                ratio = near + lead * distant
                some_ratios.append(ratio)
                some_inverses.append(inverse)
                some_leads.append(lead)
            nears.append(near)
            distants.append(distant)
            ratios.append(some_ratios)
            inverses.append(some_inverses)
            leads.append(some_leads)
        for step in range(1, lev):
            end_copy(step, (block + lev - step) % lev, n).wait_recv()
        for i_k, k in enumerate(sections):
            near, distant = nears[i_k], distants[i_k]
            value = ends[0, k, DEEP:2 * DEEP, :]
            values = [value]
            for b in range(1, lev):
                first = ends[b, k, 0:DEEP, :] + near * value
                value = ends[b, k, DEEP:2 * DEEP, :] + distant * value + leads[i_k][b] * first
                values.append(value)
            follow = zeros
            first_val[lev, k] = follow
            last_val[0, k] = follow
            for b in range(lev - 1, 0, -1):
                follow = inverses[i_k][b] * (
                    ends[b, k, 0:DEEP, :] + near * values[b - 1] + distant * follow
                )
                first_val[b, k] = follow
                last_val[b, k] = values[b - 1] + ratios[i_k][b - 1] * follow
        below = [last_val[block, k] for k in sections]

        def up_pair(j, carry):
            rows = level_rows(levels - 2 - 2 * j, 2)
            after = []
            for i_k, k in enumerate(sections):
                both, inverse = own_part[k, rows, :], coef[k, rows, :]
                high = both[DEEP:] + inverse[DEEP:] * carry[i_k]
                low = both[:DEEP] + inverse[:DEEP] * high
                gain = from_lo[k, rows, :]
                own_part[k, rows, :] = jnp.concatenate(
                    [low + gain[:DEEP] * below[i_k], high + gain[DEEP:] * below[i_k]], axis=0
                )
                after.append(low)
            return tuple(after)

        over_pairs(
            up_pair, 0, levels // 2, tuple(first_val[block + 1, k] for k in sections)
        )
        tiles = KXM // 128
        for k in sections:
            for c in range(2):
                for j in range(PER):
                    out_ref[pl.ds(c * levels * tiles + k * PER + j, levels, stride=tiles), :] = (
                        own_part[k, pl.ds(c * PER + j, levels, stride=DEEP), :]
                    )

    for n in range(len(section_groups)):
        down_pass(n)
    for n in range(len(section_groups)):
        up_pass(n)

    to_prev.wait_send()
    to_next.wait_send()

    def lines_sent(d, carry):
        for which in range(2):
            for g in range(2):
                line_copy(d, which, g).wait_send()
        return carry

    lax.fori_loop(0, chain, lines_sent, 0)

    def flows_sent(s, carry):
        d, way = unit(s)
        for k in range(SECTIONS):
            for g in range(2):
                flow_copy(d, way, k, g).wait_send()
        return carry

    lax.fori_loop(0, chain - 1, flows_sent, 0)
    for n in range(len(section_groups)):
        for step in range(1, lev):
            end_copy(step, block, n).wait_send()


def solution(mesh):
    wide, lev = mesh.shape["wide"], mesh.shape["lev"]
    tables = make_tables()

    def local(nonlinear):
        _, _, levels, rows_ky, chunk = nonlinear.shape
        rows = levels * rows_ky
        halo_rows = max(16, rows_ky)
        chain = wide // 2
        f32, bf16 = jnp.float32, jnp.bfloat16
        dma = pltpu.SemaphoreType.DMA
        pressure = pl.pallas_call(
            functools.partial(kernel, wide, lev, rows_ky, levels),
            out_shape=pltpu.VMEM((2 * levels * KXM // 128, 128), f32),
            in_specs=[
                pl.BlockSpec(memory_space=pl.ANY),
                pl.BlockSpec(memory_space=pl.ANY),
            ],
            out_specs=pl.BlockSpec(memory_space=pltpu.VMEM),
            scratch_shapes=[
                pltpu.VMEM((3, 2, rows, chunk), bf16),
                pltpu.VMEM((2 * chunk, 2 * KXM), bf16),
                pltpu.VMEM((rows_ky, 4, levels, chunk), bf16),
                pltpu.VMEM((chain, 4, levels, chunk), bf16),
                pltpu.VMEM((2, halo_rows, chunk), bf16),
                pltpu.VMEM((2, halo_rows, chunk), bf16),
                pltpu.VMEM((2, rows + 2 * rows_ky, chunk), f32),
                pltpu.VMEM((SECTIONS, levels * DEEP, 128), f32),
                pltpu.VMEM((SECTIONS, levels * DEEP, 128), f32),
                pltpu.VMEM((chain, SECTIONS, (levels + 2) * DEEP, 128), bf16),
                pltpu.VMEM((chain + 1, SECTIONS, (levels + 2) * DEEP, 128), bf16),
                pltpu.VMEM((SECTIONS, levels * DEEP, 128), f32),
                pltpu.VMEM((SECTIONS, levels * DEEP, 128), f32),
                pltpu.VMEM((lev, SECTIONS, 2 * DEEP, 128), f32),
                pltpu.VMEM((lev + 1, SECTIONS, DEEP, 128), f32),
                pltpu.VMEM((lev + 1, SECTIONS, DEEP, 128), f32),
                pltpu.VMEM((SECTIONS, 2, DEEP, 128), f32),
                dma((3, 2)),
                dma((2, 4)),
                dma((2,)),
                dma((2,)),
                dma((2, 2, chain)),
                dma((2, 2, chain)),
                dma((chain, SECTIONS, 2)),
                dma((chain + 1, SECTIONS, 2)),
                dma((lev, 2)),
                dma((lev, 2)),
            ],
            compiler_params=pltpu.CompilerParams(
                collective_id=0, has_side_effects=True, vmem_limit_bytes=56 * 2**20
            ),
            cost_estimate=pl.CostEstimate(
                flops=2 * 4 * levels * NXG * 2 * KXM,
                bytes_accessed=2 * chunk * 2 * KXM * 2 + 4 * rows * chunk * 2,
                transcendentals=0,
            ),
        )(nonlinear.reshape(3, 2, rows, chunk), jnp.asarray(tables))
        return pressure.reshape(2, levels, 1, KXM)

    placed = (P(None, None, "lev", None, "wide"),)
    return jax.shard_map(
        local, mesh=mesh, in_specs=placed, out_specs=P(None, "lev", "wide", None), check_vma=False
    )
```
